32 devices in a mesh: section: 2 (over core), dp: 16 (over z, y, x).
Axes of the slice: x: 2, y: 2, z: 4, core: 2. Of those that a mesh axis runs over, the one named last changes fastest.
Arguments:
- inputs: bfloat16 [32, 1024, 768], P('dp'), may hold values from -6 to 6
- cotangent: bfloat16 [32, 1024, 768], P('dp'), may hold values from -6 to 6
- lengths: int32 [32], P('dp'), may hold values from 1 to 1024, as said below
- mix_weight: float32 [2, 768, 2304], P('section', 'dp'), may hold values from -0.21875 to 0.21875
- out_weight: float32 [2, 768, 768], P('section', 'dp'), may hold values from -2.5 to 2.5
- up_weight: float32 [2, 768, 3072], P('section', 'dp'), may hold values from -0.21875 to 0.21875
- down_weight: float32 [2, 3072, 768], P('section', 'dp'), may hold values from -0.109375 to 0.109375
- vectors: float32 [2, 9216], P('section', 'dp'), may hold values from -2 to 3
- first_mix: float32 [2, 768, 2304], P('section', 'dp'), may hold values from -0.00018310547 to 0.00018310547
- first_out: float32 [2, 768, 768], P('section', 'dp'), may hold values from -0.00018310547 to 0.00018310547
- first_up: float32 [2, 768, 3072], P('section', 'dp'), may hold values from -0.00018310547 to 0.00018310547
- first_down: float32 [2, 3072, 768], P('section', 'dp'), may hold values from -0.00018310547 to 0.00018310547
- first_vectors: float32 [2, 9216], P('section', 'dp'), may hold values from -0.00018310547 to 0.00018310547
- second_mix: float32 [2, 768, 2304], P('section', 'dp')
- second_out: float32 [2, 768, 768], P('section', 'dp')
- second_up: float32 [2, 768, 3072], P('section', 'dp')
- second_down: float32 [2, 3072, 768], P('section', 'dp')
- second_vectors: float32 [2, 9216], P('section', 'dp')
Outputs:
- activations: bfloat16 [2, 32, 1024, 768], P('section', 'dp')
- input_grads: float32 [2, 32, 1024, 768], P('section', 'dp')
- grad_norm: float32 [], replicated
- mean_mix: float32 [2, 768, 2304], P('section', 'dp')
- square_mix: float32 [2, 768, 2304], P('section', 'dp')
- master_mix: float32 [2, 768, 2304], P('section', 'dp')
- mean_out: float32 [2, 768, 768], P('section', 'dp')
- square_out: float32 [2, 768, 768], P('section', 'dp')
- master_out: float32 [2, 768, 768], P('section', 'dp')
- mean_up: float32 [2, 768, 3072], P('section', 'dp')
- square_up: float32 [2, 768, 3072], P('section', 'dp')
- master_up: float32 [2, 768, 3072], P('section', 'dp')
- mean_down: float32 [2, 3072, 768], P('section', 'dp')
- square_down: float32 [2, 3072, 768], P('section', 'dp')
- master_down: float32 [2, 3072, 768], P('section', 'dp')
- mean_vectors: float32 [2, 9216], P('section', 'dp')
- square_vectors: float32 [2, 9216], P('section', 'dp')
- master_vectors: float32 [2, 9216], P('section', 'dp')
The draws below stay inside these ranges and needn't reach their ends.
Inputs may be any that keep to these rules, and one draw needn't show every extreme that they name: `lengths`: the first sequence of the last index of dp has exactly 1024 valid tokens.
All inputs are finite; a program needn't handle non-finite values.
Results may differ from the reference program's by a relative error of at most 0.018.
The reference program's roundings to bfloat16 on the way count: a program that leaves them out, or rounds other values in their place, can miss the bound.
Values may be sent and summed in bfloat16 or wider, within the bound.
A program may use at most 512 MiB of HBM per device.

```python
import math
import jax
import jax.numpy as jnp
from jax import lax

D = 768
FF = 3072
HEAD = 64
LEN = 1024
MICRO = 2
STEP = 10
SEQ_MB = 1
NVEC = 9216
PARAMS = 14174208
SEQS = 32


def draw_lengths(key, part):
    key = jax.random.fold_in(key, 5)
    seqs_per_device = MICRO * SEQ_MB
    devices = SEQS // seqs_per_device
    seq_index = jnp.arange(SEQS, dtype=jnp.int32)
    device = seq_index // seqs_per_device
    length_cap = LEN // 3 + (LEN - LEN // 3) * device // max(devices - 1, 1)
    uniform_pick = jax.random.randint(key, (SEQS,), 0, 1024, dtype=jnp.int32)
    square = uniform_pick * uniform_pick // 1023
    shortening = (length_cap - 1) * (square * uniform_pick // 1023) // 1023
    return jnp.where(seq_index == SEQS - seqs_per_device, LEN, length_cap - shortening).astype(jnp.int32)


def draw_vectors(key, part):
    key = jax.random.fold_in(key, 7)
    subkeys = jax.random.split(key, 3)
    position = jnp.arange(D, dtype=jnp.float32) / (D - 1)
    rising = 0.6 + 1.2 * position
    jitter = jnp.exp(0.05 * jax.random.truncated_normal(subkeys[0], -2.0, 2.0, (2, 2, D), jnp.float32))
    gain_rows = rising * jitter
    biases = 0.2 * jax.random.truncated_normal(subkeys[1], -4.0, 4.0, (2, 6, D), jnp.float32)
    up_bias = 0.3 * jax.random.truncated_normal(subkeys[2], -4.0, 4.0, (2, FF), jnp.float32)
    columns = jnp.stack([gain_rows[:, 0], biases[:, 0], biases[:, 1], biases[:, 2], biases[:, 3], gain_rows[:, 1], biases[:, 4], biases[:, 5]], axis=2)
    table = jnp.concatenate([columns, up_bias.reshape(2, D, FF // D)], axis=2)
    return table.reshape(2, NVEC)


def second_moment(key, shape):
    spread = jax.random.uniform(key, shape, jnp.float32, 0.0, math.log(4.0))
    return jnp.exp(spread) * (0.001001 / PARAMS)


def draw_second_mix(key, part):
    key = jax.random.fold_in(key, 11)
    return second_moment(key, (2, D, 3 * D))


def draw_second_out(key, part):
    key = jax.random.fold_in(key, 13)
    return second_moment(key, (2, D, D))


def draw_second_up(key, part):
    key = jax.random.fold_in(key, 17)
    return second_moment(key, (2, D, FF))


def draw_second_down(key, part):
    key = jax.random.fold_in(key, 19)
    return second_moment(key, (2, FF, D))


def draw_second_vectors(key, part):
    key = jax.random.fold_in(key, 23)
    return second_moment(key, (2, NVEC))


def steps_of(key, dims, cuts, low, largest):
    level, own = 1.0, jax.random.fold_in(key, 6)
    for dim, shards_of in cuts:
        steps = jnp.exp(jax.random.uniform(jax.random.fold_in(own, dim), (shards_of,), jnp.float32, low / len(cuts), largest / len(cuts)))
        level = level * jnp.repeat(steps, dims[dim] // shards_of).reshape([-1 if axis == dim else 1 for axis in range(len(dims))])
    return level


def noise(stream_key, extent, deviation, bound, cuts=(), held_as=jnp.bfloat16):
    loudness = steps_of(stream_key, extent, cuts, -0.22, 0.18) if cuts else 1.0
    entries = jax.random.normal(stream_key, extent, jnp.float32) * deviation * loudness
    return jnp.minimum(jnp.maximum(entries, -bound), bound).astype(held_as)


def setup_inputs(seed: int = 0) -> dict:
    arg_keys = jax.random.split(jax.random.key(seed), 19)
    return {
        "inputs": noise(arg_keys[0], (SEQS, LEN, D), 1.0, 6.0, ((0, 16),)),
        "cotangent": noise(arg_keys[1], (SEQS, LEN, D), 1.0, 6.0, ((0, 16),)),
        "lengths": draw_lengths(jax.random.fold_in(arg_keys[18], 71), 0),
        "mix_weight": noise(arg_keys[3], (2, D, 3 * D), D ** -0.5, 0.21875, ((0, 2), (1, 16)), jnp.float32),
        "out_weight": noise(arg_keys[4], (2, D, D), (D * 8 // LEN) ** -0.5, 2.5, ((0, 2), (1, 16)), jnp.float32),
        "up_weight": noise(arg_keys[5], (2, D, FF), D ** -0.5, 0.21875, ((0, 2), (1, 16)), jnp.float32),
        "down_weight": noise(arg_keys[6], (2, FF, D), FF ** -0.5, 0.109375, ((0, 2), (1, 16)), jnp.float32),
        "vectors": draw_vectors(jax.random.fold_in(arg_keys[18], 71), 0),
        "first_mix": noise(arg_keys[8], (2, D, 3 * D), (PARAMS * 81) ** -0.5, 0.00018310547, ((0, 2), (1, 16)), jnp.float32),
        "first_out": noise(arg_keys[9], (2, D, D), (PARAMS * 81) ** -0.5, 0.00018310547, ((0, 2), (1, 16)), jnp.float32),
        "first_up": noise(arg_keys[10], (2, D, FF), (PARAMS * 81) ** -0.5, 0.00018310547, ((0, 2), (1, 16)), jnp.float32),
        "first_down": noise(arg_keys[11], (2, FF, D), (PARAMS * 81) ** -0.5, 0.00018310547, ((0, 2), (1, 16)), jnp.float32),
        "first_vectors": noise(arg_keys[12], (2, NVEC), (PARAMS * 81) ** -0.5, 0.00018310547, ((0, 2), (1, 16)), jnp.float32),
        "second_mix": draw_second_mix(jax.random.fold_in(arg_keys[18], 71), 0),
        "second_out": draw_second_out(jax.random.fold_in(arg_keys[18], 71), 0),
        "second_up": draw_second_up(jax.random.fold_in(arg_keys[18], 71), 0),
        "second_down": draw_second_down(jax.random.fold_in(arg_keys[18], 71), 0),
        "second_vectors": draw_second_vectors(jax.random.fold_in(arg_keys[18], 71), 0),
    }


@jax.custom_vjp
def low(v):
    return lax.optimization_barrier(v.astype(jnp.bfloat16)).astype(jnp.float32)

@jax.custom_vjp
def low_back(v):
    return v

def low_keep(v):
    return (low(v), None)

def low_pass(kept, grad):
    return (grad,)

def back_keep(v):
    return (v, None)

def back_low(kept, grad):
    return (low(grad),)
low.defvjp(low_keep, low_pass)
low_back.defvjp(back_keep, back_low)
layer_eps = 1e-05
beta_one = 0.9
beta_two = 0.999
matrix_rate = 0.05
project_rate = 0.25
vector_rate = 0.5
decay_rate = 0.1
adam_eps = 1e-08
clip_norm = 1.0
masked_score = -1e+30
highest = lax.Precision.HIGHEST

def layer_norm(values, scale_vec, shift_vec):
    centered = values - lax.optimization_barrier(jnp.mean(values, -1, keepdims=True))
    variance = lax.optimization_barrier(jnp.mean(centered * centered, -1, keepdims=True))
    return centered * lax.rsqrt(variance + layer_eps) * scale_vec + shift_vec

def pieces(vector):
    slots = vector.reshape(D, 8 + FF // D)
    return (slots[:, 0], slots[:, 1], slots[:, 2], slots[:, 3], slots[:, 4], slots[:, 5], slots[:, 6], slots[:, 8:].reshape(FF), slots[:, 7])

def attend_sequence(queries, keys_all, values_all, length):
    head_count = D // HEAD
    query_heads = queries.reshape(LEN, head_count, HEAD)
    key_heads = keys_all.reshape(LEN, head_count, HEAD)
    value_heads = values_all.reshape(LEN, head_count, HEAD)
    block_rows = min(512, LEN)
    key_pos = jnp.arange(LEN, dtype=jnp.int32)

    def attend_block(row_start):
        query_rows = lax.dynamic_slice_in_dim(query_heads, row_start, block_rows, 0)
        raw_scores = jnp.einsum('qhe,khe->hqk', query_rows, key_heads, precision=highest)
        scores = low_back(raw_scores * 0.125)
        query_pos = row_start + jnp.arange(block_rows, dtype=jnp.int32)
        allowed = (key_pos[None, :] <= query_pos[:, None]) & (key_pos[None, :] < length)
        scores = jnp.where(allowed[None], scores, masked_score)
        row_top = lax.optimization_barrier(jnp.max(scores, -1, keepdims=True))
        exponent = jnp.exp(scores - row_top)
        probs_low = low(exponent / lax.optimization_barrier(jnp.sum(exponent, -1, keepdims=True)))
        return jnp.einsum('hqk,khe->qhe', probs_low, value_heads, precision=highest)
    starts = jnp.arange(LEN // block_rows, dtype=jnp.int32) * block_rows
    blocks = lax.map(jax.checkpoint(attend_block), starts)
    return blocks.reshape(LEN, D)

def residual_block(residual, length, params):
    mix_used, out_used, up_used, down_used, vector_used = params
    gain_one, shift_one, bias_query, bias_value, bias_out, gain_two, shift_two, bias_up, bias_down = pieces(vector_used)
    normed = low(layer_norm(residual, gain_one, shift_one))
    mixed_all = jnp.dot(normed, mix_used, precision=highest)
    queries = low_back(low(mixed_all[:, 0:D] + bias_query))
    keys_all = low_back(low(mixed_all[:, D:2 * D]))
    values_all = low_back(low(mixed_all[:, 2 * D:3 * D] + bias_value))
    context = low_back(low(attend_sequence(queries, keys_all, values_all, length)))
    attended = low_back(jnp.dot(context, out_used, precision=highest) + bias_out)
    middle = residual + attended
    normed_two = low(layer_norm(middle, gain_two, shift_two))
    hidden = low_back(jnp.dot(normed_two, up_used, precision=highest) + bias_up)
    activated = low(jax.nn.gelu(hidden, approximate=True))
    branch_out = low_back(jnp.dot(activated, down_used, precision=highest) + bias_down)
    return middle + branch_out

def adam_update(master, gradient, first_old, second_old, decay_weight, rate):
    first_new = beta_one * first_old + (1.0 - beta_one) * gradient
    second_new = beta_two * second_old + (1.0 - beta_two) * gradient * gradient
    first_hat = first_new / (1.0 - beta_one ** STEP)
    second_hat = second_new / (1.0 - beta_two ** STEP)
    updated = master - rate * (first_hat / (jnp.sqrt(second_hat) + adam_eps) + decay_weight * master)
    return (first_new, second_new, updated)

def reference(inputs, cotangent, lengths, mix_weight, out_weight, up_weight, down_weight, vectors, first_mix, first_out, first_up, first_down, first_vectors, second_mix, second_out, second_up, second_down, second_vectors):
    inputs_f = inputs.astype(jnp.float32)
    cot_f = cotangent.astype(jnp.float32)
    zeros_f = jnp.zeros_like(inputs_f)
    masters = (mix_weight, out_weight, up_weight, down_weight, vectors)

    def total_loss(inputs_in, zeros_in, master_set):
        used = tuple((low(master_item) for master_item in master_set))
        layer_zero = tuple((master_item[0] for master_item in used))
        layer_one = tuple((master_item[1] for master_item in used))

        def sequence_loss(input_row, zero_row, length, cot_row):
            layer_output = residual_block(input_row, length, layer_zero)
            passed = low_back(low(layer_output)) + zero_row
            final = residual_block(passed, length, layer_one)
            row_mask = (jnp.arange(LEN, dtype=jnp.int32) < length).astype(jnp.float32)
            loss_part = jnp.sum(final * cot_row * row_mask[:, None])
            return (loss_part, (passed, final))
        checked = jax.checkpoint(sequence_loss)

        def scan_step(loss_sum, sequence_item):
            loss_part, kept_rows = checked(*sequence_item)
            return (loss_sum + loss_part, kept_rows)
        loss_total, kept_rows = lax.scan(scan_step, jnp.zeros((), jnp.float32), (inputs_in, zeros_in, lengths, cot_f))
        return (loss_total, kept_rows)
    loss_total, pullback, kept_rows = jax.vjp(total_loss, inputs_f, zeros_f, masters, has_aux=True)
    grad_inputs, grad_passed, grads = pullback(jnp.ones((), jnp.float32))
    passed, final = kept_rows
    activations = jnp.stack([passed, final]).astype(jnp.bfloat16)
    input_grads = jnp.stack([grad_inputs, grad_passed])
    square_total = sum((jnp.sum(gradient * gradient) for gradient in grads))
    grad_norm = jnp.sqrt(square_total)
    factor = jnp.minimum(1.0, clip_norm / (grad_norm + 1e-06))
    mean_mix, square_mix, master_mix = adam_update(mix_weight, grads[0] * factor, first_mix, second_mix, decay_rate, matrix_rate)
    mean_out, square_out, master_out = adam_update(out_weight, grads[1] * factor, first_out, second_out, decay_rate, project_rate)
    mean_up, square_up, master_up = adam_update(up_weight, grads[2] * factor, first_up, second_up, decay_rate, matrix_rate)
    mean_down, square_down, master_down = adam_update(down_weight, grads[3] * factor, first_down, second_down, decay_rate, matrix_rate)
    mean_vectors, square_vectors, master_vectors = adam_update(vectors, grads[4] * factor, first_vectors, second_vectors, 0.0, vector_rate)
    return (activations, input_grads, grad_norm, mean_mix, square_mix, master_mix, mean_out, square_out, master_out, mean_up, square_up, master_up, mean_down, square_down, master_down, mean_vectors, square_vectors, master_vectors)
```

```python
import jax, jax.numpy as jnp
from jax import lax
from jax.experimental import pallas as pl
from jax.experimental.pallas import tpu as pltpu
from jax.sharding import PartitionSpec as P
D=768; FF=3072; LEN=1024; RB=256; NB=LEN//RB; FB=768
f32=jnp.float32; bf16=jnp.bfloat16
NT=(((1,),(1,)),((),())); TN=(((0,),(0,)),((),()))
def nn(a,b): return jnp.dot(a,b,preferred_element_type=f32)
def nt(a,b): return lax.dot_general(a,b,NT,preferred_element_type=f32)
def tn(a,b): return lax.dot_general(a,b,TN,preferred_element_type=f32)
K0=0.7978845608028654; K1=0.044715
def rows_of(i): return pl.ds(pl.multiple_of(i*RB,RB),RB)
def norm_parts(v):
    cen=v-jnp.mean(v,-1,keepdims=True)
    rstd=lax.rsqrt(jnp.mean(cen*cen,-1,keepdims=True)+1e-5)
    return cen*rstd, rstd
def fwd_body(length, x, mix, out, up, down, vec, bup, y, q, k, v, ctx, lse, mid, act, dg, ready, done):
    ready('mix')
    def st1(i,_):
        r=rows_of(i)
        xh,_r=norm_parts(x[r,:].astype(f32))
        a=(xh*vec[0:1,:]+vec[1:2,:]).astype(bf16)
        q[r,:]=((nn(a,mix[:,0:D])+vec[2:3,:]).astype(bf16).astype(f32)*0.125).astype(bf16)
        k[r,:]=nn(a,mix[:,D:2*D]).astype(bf16)
        v[r,:]=(nn(a,mix[:,2*D:3*D])+vec[3:4,:]).astype(bf16)
        return 0
    lax.fori_loop(0,NB,st1,0)
    done((1,2,3))
    kb=jnp.where(lax.broadcasted_iota(jnp.int32,(1,LEN),1)<length,0.0,-1e30).astype(f32)
    tri=lax.broadcasted_iota(jnp.int32,(RB,RB),1)<=lax.broadcasted_iota(jnp.int32,(RB,RB),0)
    lane=lax.broadcasted_iota(jnp.int32,(RB,128),1)
    def att(p,_):
        c=pl.ds(pl.multiple_of(p*128,128),128)
        for i in range(NB):
            lo=i*RB; r=slice(lo,lo+RB)
            qp=q[r,c]; outs=[]; ls=[]
            for h in range(2):
                qh=jnp.where((lane<64)==(h==0),qp,jnp.zeros_like(qp))
                sd=jnp.where(tri,nt(qh,k[r,c])+kb[:,lo:lo+RB],-1e30)
                m=jnp.max(sd,-1,keepdims=True)
                if i:
                    sl=nt(qh,k[0:lo,c])+kb[:,0:lo]
                    m=jnp.maximum(m,jnp.max(sl,-1,keepdims=True))
                ed=jnp.exp(sd-m); tot=jnp.sum(ed,-1,keepdims=True)
                o=nn(ed.astype(bf16),v[r,c])
                if i:
                    el=jnp.exp(sl-m); tot=tot+jnp.sum(el,-1,keepdims=True)
                    o=o+nn(el.astype(bf16),v[0:lo,c])
                outs.append(o*(1.0/tot)); ls.append(m+jnp.log(tot))
            ctx[r,c]=jnp.where(lane<64,outs[0],outs[1]).astype(bf16)
            lse[r,:]=jnp.where(lane==2*p,ls[0],jnp.where(lane==2*p+1,ls[1],lse[r,:]))
        return 0
    lse[...]=jnp.zeros_like(lse)
    lax.fori_loop(0,D//128,att,0)
    done((4,5))
    for n in ('out','up','down'): ready(n)
    def st3(i,_):
        r=rows_of(i)
        md=x[r,:].astype(f32)+nn(ctx[r,:],out[...])+vec[4:5,:]
        mid[r,:]=md
        xh,_r=norm_parts(md)
        c=(xh*vec[5:6,:]+vec[6:7,:]).astype(bf16)
        acc=md+vec[7:8,:]
        for j in range(FF//FB):
            cc=slice(j*FB,(j+1)*FB)
            h=nn(c,up[:,cc])+bup[:,cc]
            h2=h*h
            t=jnp.tanh(h*(K0+(K0*K1)*h2))
            half=0.5+0.5*t
            ab=(h*half).astype(bf16)
            act[r,cc]=ab
            dg[r,cc]=(half+(0.5*h)*(1.0-t*t)*(K0+(3*K0*K1)*h2)).astype(bf16)
            acc=acc+nn(ab,down[cc,:])
        y[r,:]=acc.astype(bf16)
        return 0
    lax.fori_loop(0,NB,st3,0)
    done((0,6,7,8))

def bwd_body(length, g, x, mix, out, up, down, vec, q, k, v, ctx, lse, mid, act, dg,
             dx, dxb, gmix, gout, gup, gdown, gvec, gbup, dh, gm, ga, cbuf, dctx, dm, dkT, dvT, stage, ssem, ready=lambda n: None):
    gvec[...]=jnp.zeros_like(gvec); gbup[...]=jnp.zeros_like(gbup)
    def cs(t): return jnp.sum(t,0,keepdims=True)
    def st1(i,_):
        r=rows_of(i)
        gb=g[r,:]; gf=gb.astype(f32)
        dc=jnp.zeros((RB,D),f32)
        for j in range(FF//FB):
            cc=slice(j*FB,(j+1)*FB)
            d=(nt(gb,down[cc,:])*dg[r,cc].astype(f32)).astype(bf16)
            dh[r,cc]=d
            gbup[0:1,cc]+=cs(d.astype(f32))
            dc=dc+nt(d,up[:,cc])
        xh,rstd=norm_parts(mid[r,:])
        cbuf[r,:]=(xh*vec[5:6,:]+vec[6:7,:]).astype(bf16)
        e=dc*vec[5:6,:]
        gmv=gf+(e-jnp.mean(e,-1,keepdims=True)-xh*jnp.mean(e*xh,-1,keepdims=True))*rstd
        gm[r,:]=gmv
        gav=gmv.astype(bf16); ga[r,:]=gav
        gvec[4:5,:]+=cs(gav.astype(f32)); gvec[5:6,:]+=cs(dc*xh); gvec[6:7,:]+=cs(dc); gvec[7:8,:]+=cs(gf)
        dctx[r,:]=nt(gav,out[...]).astype(bf16)
        return 0
    lax.fori_loop(0,NB,st1,0)
    for n in ('q','k','v','lse'): ready(n)
    kb=jnp.where(lax.broadcasted_iota(jnp.int32,(1,LEN),1)<length,0.0,-1e30).astype(f32)
    tri=lax.broadcasted_iota(jnp.int32,(RB,RB),1)<=lax.broadcasted_iota(jnp.int32,(RB,RB),0)
    lane=lax.broadcasted_iota(jnp.int32,(RB,128),1)
    lanek=lax.broadcasted_iota(jnp.int32,(LEN,128),1)
    def att(p,_):
        c=pl.ds(pl.multiple_of(p*128,128),128)
        dkT[...]=jnp.zeros_like(dkT); dvT[...]=jnp.zeros_like(dvT)
        for i in range(NB):
            lo=i*RB; r=slice(lo,lo+RB)
            qp=q[r,c]; dcp=dctx[r,c]; lr=lse[r,:]
            qT=qp.astype(f32).T.astype(bf16); dcT=dcp.astype(f32).T.astype(bf16)
            dq=None
            for h in range(2):
                sel=(lane<64)==(h==0)
                qh=jnp.where(sel,qp,jnp.zeros_like(qp)); dch=jnp.where(sel,dcp,jnp.zeros_like(dcp))
                ls=jnp.sum(jnp.where(lane==2*p+h,lr,0.0),-1,keepdims=True)
                hs=slice(h*64,h*64+64)
                pd=jnp.exp(jnp.where(tri,nt(qh,k[r,c])+kb[:,lo:lo+RB],-1e30)-ls)
                dpd=nt(dch,v[r,c])
                delta=jnp.sum(pd*dpd,-1,keepdims=True)
                if i:
                    plft=jnp.exp(nt(qh,k[0:lo,c])+kb[:,0:lo]-ls)
                    dpl=nt(dch,v[0:lo,c])
                    delta=delta+jnp.sum(plft*dpl,-1,keepdims=True)
                dsd=(pd*(dpd-delta)).astype(bf16)
                dkT[hs,r]+=nn(qT[hs],dsd); dvT[hs,r]+=nn(dcT[hs],pd.astype(bf16))
                t=nn(dsd,k[r,c])
                if i:
                    dsl=(plft*(dpl-delta)).astype(bf16)
                    dkT[hs,0:lo]+=nn(qT[hs],dsl); dvT[hs,0:lo]+=nn(dcT[hs],plft.astype(bf16))
                    t=t+nn(dsl,k[0:lo,c])
                dq=t if h==0 else jnp.where(lane<64,dq,t)
            dm[r,c]=(dq*0.125).astype(bf16)
        dm[:,pl.ds(pl.multiple_of(D+p*128,128),128)]=dkT[...].T.astype(bf16)
        dm[:,pl.ds(pl.multiple_of(2*D+p*128,128),128)]=dvT[...].T.astype(bf16)
        return 0
    lax.fori_loop(0,D//128,att,0)
    def put(n,dst,val):
        slot=n%2
        def cp(): return pltpu.make_async_copy(stage.at[slot],dst,ssem.at[slot])
        @pl.when(n>=2)
        def _(): cp().wait()
        stage[slot]=val
        cp().start()
    ready("act")
    def gd(m,_):
        rr=rows_of(m)
        put(m,gdown.at[rr,:],tn(act[:,rr],g[...]).astype(bf16)); return 0
    lax.fori_loop(0,FF//RB,gd,0)
    def gu(m,_):
        rr=rows_of(m)
        for j in range(FF//FB):
            cc=slice(j*FB,(j+1)*FB)
            put(12+4*m+j,gup.at[rr,cc],tn(cbuf[:,rr],dh[:,cc]).astype(bf16))
        return 0
    lax.fori_loop(0,D//RB,gu,0)
    ready("ctx")
    for t in range(3):
        rr=slice(t*256,t*256+256)
        put(24+t,gout.at[rr,:],tn(ctx[:,rr],ga[...]).astype(bf16))
    ready("x"); ready("mix")
    def st3(i,_):
        r=rows_of(i)
        d=dm[r,:]; df=d.astype(f32)
        gvec[2:3,:]+=cs(df[:,0:D]); gvec[3:4,:]+=cs(df[:,2*D:])
        da=nt(d,mix[...])
        xh,rstd=norm_parts(x[r,:].astype(f32))
        cbuf[r,:]=(xh*vec[0:1,:]+vec[1:2,:]).astype(bf16)
        gvec[0:1,:]+=cs(da*xh); gvec[1:2,:]+=cs(da)
        e=da*vec[0:1,:]
        o=gm[r,:]+(e-jnp.mean(e,-1,keepdims=True)-xh*jnp.mean(e*xh,-1,keepdims=True))*rstd
        dx[r,:]=o; dxb[r,:]=o.astype(bf16)
        return 0
    lax.fori_loop(0,NB,st3,0)
    def gmx(m,_):
        rr=rows_of(m)
        for j in range(3):
            cc=slice(j*D,(j+1)*D)
            put(27+3*m+j,gmix.at[rr,cc],tn(cbuf[:,rr],dm[:,cc]).astype(bf16))
        return 0
    lax.fori_loop(0,D//RB,gmx,0)
    for n in (34,35): pltpu.make_async_copy(stage.at[n%2],gmix.at[rows_of(2),0:D],ssem.at[n%2]).wait()

VM = pl.BlockSpec(memory_space=pltpu.VMEM)
SM = pl.BlockSpec(memory_space=pltpu.SMEM)
AN = pl.BlockSpec(memory_space=pl.ANY)
MESH = pl.DeviceIdType.MESH
MIB = 2**20
STEP = 10
TABLE = 8 + FF // D


def S(shape, dtype):
    return jax.ShapeDtypeStruct(shape, dtype)


def vm_like(items):
    return [pltpu.VMEM(i.shape, i.dtype) for i in items]


def layer_fwd(layer, length, x, weights, table, bup):
    wn = ["mix", "out", "up", "down"]
    saved = [S((LEN, D), bf16)] * 5 + [S((LEN, 128), f32), S((LEN, D), f32), S((LEN, FF), bf16), S((LEN, FF), bf16)]
    wsc = [S(w.shape[1:], w.dtype) for w in weights]

    def kern(l, vec, bup, x_h, *refs):
        wh, oh = refs[:4], refs[4:13]
        x_v, wv, ov = refs[13], refs[14:18], refs[18:27]
        lsem, ssem = refs[27:]
        cps = [pltpu.make_async_copy(x_h, x_v, lsem.at[0])]
        cps += [pltpu.make_async_copy(wh[i].at[layer], wv[i], lsem.at[1 + i]) for i in range(4)]
        for c in cps:
            c.start()
        cps[0].wait()

        def ready(n):
            cps[1 + wn.index(n)].wait()

        sends = [pltpu.make_async_copy(ov[i], oh[i], ssem.at[i]) for i in range(9)]

        def done(which):
            for i in which:
                sends[i].start()

        fwd_body(l[0], x_v, *wv, vec, bup, *ov, ready=ready, done=done)
        for c in sends:
            c.wait()

    return pl.pallas_call(
        kern,
        out_shape=saved,
        in_specs=[SM, VM, VM] + [AN] * 5,
        out_specs=[AN] * 9,
        scratch_shapes=vm_like([x] + wsc + saved) + [pltpu.SemaphoreType.DMA((5,)), pltpu.SemaphoreType.DMA((9,))],
        compiler_params=pltpu.CompilerParams(vmem_limit_bytes=60 * MIB),
        name="layer_fwd",
    )(length, table, bup, x, *weights)


def layer_bwd(layer, length, g, x, weights, table, saved):
    names = ["g", "dg", "down", "up", "mid", "out", "q", "k", "v", "lse", "act", "ctx", "x", "mix"]
    q, k, v, ctx, lse, mid, act, dg = saved
    mix, out, up, down = weights
    vals = dict(g=g, dg=dg, down=down, up=up, mid=mid, out=out, q=q, k=k, v=v, lse=lse, act=act, ctx=ctx, x=x, mix=mix)
    wn = ("mix", "out", "up", "down")
    arrs = [vals[n] for n in names]
    hold = [S(vals[n].shape[1:] if n in wn else vals[n].shape, vals[n].dtype) for n in names]

    def kern(l, vec, *refs):
        n = len(names)
        hb = dict(zip(names, refs[:n]))
        outs = refs[n : n + 8]
        refs = refs[n + 8 :]
        vm = dict(zip(names, refs[:n]))
        lsem, scr = refs[n], refs[n + 1 :]
        cps = {
            nm: pltpu.make_async_copy(hb[nm].at[layer] if nm in wn else hb[nm], vm[nm], lsem.at[i])
            for i, nm in enumerate(names)
        }
        for nm in names:
            cps[nm].start()

        def ready(nm):
            cps[nm].wait()

        for nm in names[:6]:
            ready(nm)
        bwd_body(
            l[0], vm["g"], vm["x"], vm["mix"], vm["out"], vm["up"], vm["down"], vec,
            vm["q"], vm["k"], vm["v"], vm["ctx"], vm["lse"], vm["mid"], vm["act"], vm["dg"],
            *outs, vm["dg"], *scr, ready=ready,
        )

    return pl.pallas_call(
        kern,
        out_shape=[S((LEN, D), f32), S((LEN, D), bf16), S((D, 3 * D), bf16), S((D, D), bf16), S((D, FF), bf16), S((FF, D), bf16), S((8, D), f32), S((8, FF), f32)],
        in_specs=[SM, VM] + [AN] * 14,
        out_specs=[VM] * 2 + [AN] * 4 + [VM] * 2,
        scratch_shapes=vm_like(hold) + [pltpu.SemaphoreType.DMA((14,))]
        + vm_like([S((LEN, D), f32)] + [S((LEN, D), bf16)] * 3 + [S((LEN, 3 * D), bf16)] + [S((128, LEN), f32)] * 2 + [S((2, RB, D), bf16)])
        + [pltpu.SemaphoreType.DMA((2,))],
        compiler_params=pltpu.CompilerParams(vmem_limit_bytes=63 * MIB),
        name="layer_bwd",
    )(length, table, *arrs)


ZS, YS, XS = 4, 2, 2


def place():
    s = lax.axis_index("section")
    d = lax.axis_index("dp")
    return s, d // (YS * XS), (d // XS) % YS, d % XS


def at_chip(s, z, y, x):
    return (s, z * (YS * XS) + y * XS + x)


def partners(s, z, y, x):
    others = [at_chip(1 - s, z, y, x), at_chip(s, z, y, 1 - x), at_chip(s, z, 1 - y, x)]
    return others + [at_chip(s, (z + r) % ZS, y, x) for r in range(1, ZS)]


def greet(devices):
    barrier = pltpu.get_barrier_semaphore()
    for dev in devices:
        pl.semaphore_signal(barrier, inc=1, device_id=dev, device_id_type=MESH)
    pl.semaphore_wait(barrier, len(devices))


def gather_weights(shards):
    n = len(shards)
    half = ZS // 2

    def kern(*refs):
        src, full, own = refs[:n], refs[n : 2 * n], refs[2 * n : 3 * n]
        send, recv, loc = refs[3 * n :]
        s, z, y, x = place()
        near = partners(s, z, y, x)
        sib, px, py, pz = near[0], near[1], near[2], near[3:]
        greet(near)
        lo, hi = slice(0, half), slice(half, ZS)

        def copy(a, slot, idx, dev, source=None):
            dst = full[a].at[idx]
            return pltpu.make_async_remote_copy(
                src_ref=dst if source is None else source, dst_ref=dst, send_sem=send.at[a, slot],
                recv_sem=recv.at[a, slot], device_id=dev, device_id_type=MESH)

        def local(a):
            return pltpu.make_async_copy(own[a], full[a].at[s, z, y, x], loc.at[a])

        def first(a):
            own[a][...] = src[a][...].astype(bf16)
            local(a).start()
            for r in range(1, ZS):
                copy(a, r - 1, (s, z, y, x), pz[r - 1], own[a]).start()

        def wait_first(a):
            for r in range(1, ZS):
                copy(a, r - 1, (s, (z - r) % ZS, y, x), pz[r - 1]).wait_recv()
            local(a).wait()

        second_out = [(3, (s, lo, y, x), px), (4, (s, hi, y, x), py)]
        second_in = [(3, (s, lo, y, 1 - x), px), (4, (s, hi, 1 - y, x), py)]
        third_out = [(5, (s, lo, y), py), (6, (s, hi, slice(None), x), px)]
        third_in = [(5, (s, lo, 1 - y), py), (6, (s, hi, slice(None), 1 - x), px)]

        def waves(l):
            return [
                [(7, (l, slice(None), y, x), sib)],
                [(8, (l, lo, y, 1 - x), sib), (9, (l, hi, 1 - y, x), sib)],
                [(10, (l, lo, 1 - y), sib), (11, (l, hi, slice(None), 1 - x), sib)],
            ]

        def second(a):
            wait_first(a)
            for c in second_out + waves(s)[0]:
                copy(a, *c).start()

        def third(a):
            for c in second_in:
                copy(a, *c).wait_recv()
            for c in third_out + waves(s)[1]:
                copy(a, *c).start()

        def last(a):
            for c in third_in:
                copy(a, *c).wait_recv()
            for c in waves(s)[2]:
                copy(a, *c).start()

        stages = (first, second, third, last)
        for t in range(n + 3):
            for k, stage in enumerate(stages):
                if 0 <= t - k < n:
                    stage(t - k)
        for a in range(n):
            for wave in waves(1 - s):
                for c in wave:
                    copy(a, *c).wait_recv()
            for r in range(1, ZS):
                copy(a, r - 1, (s, z, y, x), pz[r - 1], own[a]).wait_send()
            for c in second_out + third_out + sum(waves(s), []):
                copy(a, *c).wait_send()

    outs = [S((2, ZS, YS, XS) + w.shape, bf16) for w in shards]
    return pl.pallas_call(
        kern,
        out_shape=outs,
        in_specs=[VM] * n,
        out_specs=[AN] * n,
        scratch_shapes=[pltpu.VMEM(w.shape, bf16) for w in shards]
        + [pltpu.SemaphoreType.DMA((n, 12)), pltpu.SemaphoreType.DMA((n, 12)), pltpu.SemaphoreType.DMA((n,))],
        compiler_params=pltpu.CompilerParams(collective_id=1, has_side_effects=True, vmem_limit_bytes=32 * MIB),
        name="gather_weights",
    )(*shards)


def scatter_grads(grads0, grads1):
    n = len(grads0)
    half = ZS // 2
    blocks = [g.shape[3:] for g in grads0]

    def kern(*refs):
        g0, g1 = refs[:n], refs[n : 2 * n]
        outs, total = refs[2 * n : 3 * n], refs[3 * n]
        refs = refs[3 * n + 1 :]
        own, sibs, a2, b2, a3, b3, r4 = [refs[i * n : (i + 1) * n] for i in range(7)]
        norms, send, recv, loc, nsend, nrecv = refs[7 * n :]
        s, z, y, x = place()
        near = partners(s, z, y, x)
        sib, px, py, pz = near[0], near[1], near[2], near[3:]
        greet(near)
        lo, hi = slice(0, half), slice(half, ZS)

        def copy(a, slot, src, dst, dev):
            return pltpu.make_async_remote_copy(
                src_ref=src, dst_ref=dst, send_sem=send.at[a, slot], recv_sem=recv.at[a, slot],
                device_id=dev, device_id_type=MESH)

        def to_sib(a, src):
            return copy(a, 0, src[a], sibs[a], sib)

        def local(a, src):
            return pltpu.make_async_copy(src[a], own[a], loc.at[a])

        for core, mine, other in ((0, g0, g1), (1, g1, g0)):
            @pl.when(s == core)
            def _():
                for a in range(n):
                    local(a, mine).start()
                    to_sib(a, other).start()

        def add(ref, idx, other, oidx):
            ref[idx] = (ref[idx].astype(f32) + other[oidx].astype(f32)).astype(ref.dtype)

        def second(a):
            return [copy(a, 1, own[a].at[lo, 1 - y], a2[a], py), copy(a, 2, own[a].at[hi, :, 1 - x], b2[a], px)]

        def third(a):
            return [copy(a, 3, own[a].at[lo, y, 1 - x], a3[a], px), copy(a, 4, own[a].at[hi, 1 - y, x], b3[a], py)]

        def fourth(a):
            return [copy(a, 4 + r, own[a].at[(z + r) % ZS, y, x], r4[a].at[r - 1], pz[r - 1]) for r in range(1, ZS)]

        def one(a):
            local(a, g0).wait()
            to_sib(a, g0).wait_recv()

            def step(i, _):
                idx = (i // (YS * XS), (i // XS) % YS, i % XS)
                add(own[a], idx, sibs[a], idx)
                return 0

            lax.fori_loop(0, ZS * YS * XS, step, 0)
            for c in second(a):
                c.start()

        def two(a):
            for c in second(a):
                c.wait()

            def step(i, _):
                h, j = i // 2, i % 2
                add(own[a], (h, y, j), a2[a], (h, j))
                add(own[a], (half + h, j, x), b2[a], (h, j))
                return 0

            lax.fori_loop(0, half * 2, step, 0)
            for c in third(a):
                c.start()

        def three(a):
            for c in third(a):
                c.wait()

            def step(h, _):
                add(own[a], (h, y, x), a3[a], (h,))
                add(own[a], (half + h, y, x), b3[a], (h,))
                return 0

            lax.fori_loop(0, half, step, 0)
            for c in fourth(a):
                c.start()

        def four(a):
            for c in fourth(a):
                c.wait()
            v = own[a][z, y, x].astype(f32)
            for r in range(ZS - 1):
                v = v + r4[a][r].astype(f32)
            outs[a][...] = v
            return jnp.sum(v * v)

        square = jnp.zeros((), f32)
        stages = (one, two, three, four)
        for t in range(n + 3):
            for k, stage in enumerate(stages):
                if 0 <= t - k < n:
                    got = stage(t - k)
                    if k == 3:
                        square = square + got
        for a in range(n):
            to_sib(a, g0).wait_send()

        def shared(k, dev, slot):
            return pltpu.make_async_remote_copy(
                src_ref=norms.at[k], dst_ref=norms.at[slot], send_sem=nsend.at[slot], recv_sem=nrecv.at[slot],
                device_id=dev, device_id_type=MESH)

        norms[0] = jnp.zeros((8, 128), f32) + square
        for k, dev in enumerate((sib, px, py)):
            c = shared(2 * k, dev, 2 * k + 1)
            c.start()
            c.wait()
            norms[2 * k + 2] = norms[2 * k] + norms[2 * k + 1]
        cs = [shared(6, pz[r], 7 + r) for r in range(ZS - 1)]
        for c in cs:
            c.start()
        for c in cs:
            c.wait()
        total[...] = norms[6] + norms[7] + norms[8] + norms[9]

    def buf(lead, a):
        return pltpu.VMEM(lead + blocks[a], grads0[a].dtype)

    scratch = []
    for lead in ((ZS, YS, XS), (ZS, YS, XS), (half, XS), (half, YS), (half,), (half,), (ZS - 1,)):
        scratch += [buf(lead, a) for a in range(n)]
    return pl.pallas_call(
        kern,
        out_shape=[S(b, f32) for b in blocks] + [S((8, 128), f32)],
        in_specs=[AN] * (2 * n),
        out_specs=[VM] * (n + 1),
        scratch_shapes=scratch
        + [pltpu.VMEM((10, 8, 128), f32), pltpu.SemaphoreType.DMA((n, 8)), pltpu.SemaphoreType.DMA((n, 8)), pltpu.SemaphoreType.DMA((n,)),
           pltpu.SemaphoreType.DMA((10,)), pltpu.SemaphoreType.DMA((10,))],
        compiler_params=pltpu.CompilerParams(collective_id=2, has_side_effects=True, vmem_limit_bytes=60 * MIB),
        name="scatter_grads",
    )(*grads0, *grads1)


RATES = (0.05, 0.25, 0.05, 0.05, 0.5)
DECAYS = (0.1, 0.1, 0.1, 0.1, 0.0)


def adam(total, grads, masters, firsts, seconds):
    n = len(grads)
    flat = [a for four in zip(grads, masters, firsts, seconds) for a in four]
    steps = 6

    def spec(a):
        if a.shape[0] % (8 * steps):
            return pl.BlockSpec(a.shape, lambda i: (0, 0))
        return pl.BlockSpec((a.shape[0] // steps, a.shape[1]), lambda i: (i, 0))

    def kern(t, *refs):
        norm = jnp.sqrt(t[0:1, 0:1])
        factor = jnp.minimum(1.0, 1.0 / (norm + 1e-06))
        for i in range(n):
            gr, w, m, u = (r[...] for r in refs[4 * i : 4 * i + 4])
            mo, uo, wo = refs[4 * n + 3 * i : 4 * n + 3 * i + 3]
            gr = gr * factor
            m1 = 0.9 * m + (1.0 - 0.9) * gr
            u1 = 0.999 * u + (1.0 - 0.999) * gr * gr
            mh = m1 / (1.0 - 0.9**STEP)
            uh = u1 / (1.0 - 0.999**STEP)
            mo[...] = m1
            uo[...] = u1
            wo[...] = w - RATES[i] * (mh / (jnp.sqrt(uh) + 1e-08) + DECAYS[i] * w)

    outs = [S(a.shape, f32) for a in masters for _ in range(3)]
    return pl.pallas_call(
        kern,
        grid=(steps,),
        out_shape=outs,
        in_specs=[pl.BlockSpec((8, 128), lambda i: (0, 0))] + [spec(a) for a in flat],
        out_specs=[spec(a) for a in outs],
        compiler_params=pltpu.CompilerParams(vmem_limit_bytes=32 * MIB),
        name="adam",
    )(total, *flat)


def swap(v):
    return lax.ppermute(v, "section", [(0, 1), (1, 0)])


def on_device(inputs, cotangent, lengths, mix, out, up, down, vectors, *moments):
    s = lax.axis_index("section")
    n_dp = lax.axis_size("dp")
    custom = n_dp == ZS * YS * XS
    masters = [m[0] for m in (mix, out, up, down)] + [vectors]
    firsts = [m[0] for m in moments[:4]] + [moments[4]]
    seconds = [m[0] for m in moments[5:9]] + [moments[9]]
    part = vectors.shape[1]
    if custom:
        padded = jnp.pad(vectors, ((0, 0), (0, 2048 - part))).reshape(16, 128)
        full = gather_weights(masters[:4] + [padded])
        weights = [w.reshape(2, -1, w.shape[-1]) for w in full[:4]]
        vecs = full[4].reshape(2, n_dp, 2048)[:, :, :part].reshape(2, -1).astype(f32)
    else:
        full = [lax.all_gather(m.astype(bf16), "dp", axis=0, tiled=True) for m in masters[:4]]
        full.append(lax.all_gather(vectors[0].astype(bf16), "dp", axis=0, tiled=True))
        full = [jnp.where(s == 0, jnp.stack([w, o]), jnp.stack([o, w])) for w, o in ((w, swap(w)) for w in full)]
        weights = full[:4]
        vecs = full[4].astype(f32)
    slots = vecs.reshape(2, D, TABLE)
    tables = slots[:, :, :8].transpose(0, 2, 1)
    bups = slots[:, :, 8:].reshape(2, 1, FF)
    length = lax.dynamic_slice_in_dim(lengths, s, 1)
    x0 = lax.dynamic_index_in_dim(inputs, s, 0, keepdims=False)
    cot = lax.dynamic_index_in_dim(cotangent, s, 0, keepdims=False)
    g1 = jnp.where(jnp.arange(LEN, dtype=jnp.int32)[:, None] < length[0], cot, jnp.zeros_like(cot))
    passed, *saved0 = layer_fwd(0, length, x0, weights, tables[0], bups[0])
    final, *saved1 = layer_fwd(1, length, passed, weights, tables[1], bups[1])
    other = swap(jnp.where(s == 0, final, passed))
    activations = jnp.where(s == 0, jnp.stack([passed, other]), jnp.stack([other, final]))[None]
    dx1, g0, *grads1 = layer_bwd(1, length, g1, passed, weights, tables[1], saved1)
    dx0, _, *grads0 = layer_bwd(0, length, g0, x0, weights, tables[0], saved0)
    other = swap(jnp.where(s == 0, dx1, dx0))
    input_grads = jnp.where(s == 0, jnp.stack([dx0, other]), jnp.stack([other, dx1]))[None]

    def vector_grads(gvec, gbup):
        return jnp.concatenate([gvec.T, gbup[0].reshape(D, FF // D)], 1).reshape(-1)

    vec_grads = [vector_grads(*g[4:]) for g in (grads0, grads1)]
    if custom:
        packed = [
            [g.reshape(ZS, YS, XS, -1, g.shape[-1]) for g in gs[:4]]
            + [jnp.pad(v.reshape(n_dp, part), ((0, 0), (0, 1024 - part))).reshape(ZS, YS, XS, 8, 128)]
            for gs, v in ((grads0, vec_grads[0]), (grads1, vec_grads[1]))
        ]
        *shards, total = scatter_grads(*packed)
        shards[4] = shards[4].reshape(1, 1024)[:, :part]
    else:
        shards = []
        for g0_, g1_ in list(zip(grads0[:4], grads1[:4])) + [tuple(vec_grads)]:
            g0_, g1_ = g0_.astype(f32), g1_.astype(f32)
            both = jnp.where(s == 0, g0_, g1_) + swap(jnp.where(s == 0, g1_, g0_))
            shards.append(lax.psum_scatter(both, "dp", scatter_dimension=0, tiled=True))
        shards[4] = shards[4][None]
        total = jnp.full((8, 128), lax.psum(sum(jnp.sum(g * g) for g in shards), ("section", "dp")))
    results = adam(total, shards, masters, firsts, seconds)
    results = [r if i >= 12 else r[None] for i, r in enumerate(results)]
    return (activations, input_grads, jnp.sqrt(total[0, 0])) + tuple(results)


def solution(mesh):
    rows = P("dp", None, None)
    mats = (P("section", "dp", None),) * 4
    vec = (P("section", "dp"),)
    acts = P("section", "dp", None, None)
    return jax.shard_map(
        on_device,
        mesh=mesh,
        in_specs=(rows, rows, P("dp")) + (mats + vec) * 3,
        out_specs=(acts, acts, P()) + (P("section", "dp", None),) * 12 + vec * 3,
        check_vma=False,
    )
```

```python
import jax, jax.numpy as jnp
from jax import lax
from jax.experimental import pallas as pl
from jax.experimental.pallas import tpu as pltpu
from jax.sharding import PartitionSpec as P
D=768; FF=3072; LEN=1024; RB=256; NB=LEN//RB; FB=768
f32=jnp.float32; bf16=jnp.bfloat16
NT=(((1,),(1,)),((),())); TN=(((0,),(0,)),((),()))
def nn(a,b): return jnp.dot(a,b,preferred_element_type=f32)
def nt(a,b): return lax.dot_general(a,b,NT,preferred_element_type=f32)
def tn(a,b): return lax.dot_general(a,b,TN,preferred_element_type=f32)
K0=0.7978845608028654; K1=0.044715
def rows_of(i): return pl.ds(pl.multiple_of(i*RB,RB),RB)
def norm_parts(v):
    cen=v-jnp.mean(v,-1,keepdims=True)
    rstd=lax.rsqrt(jnp.mean(cen*cen,-1,keepdims=True)+1e-5)
    return cen*rstd, rstd
def bwd_body(length, g, x, wq, wk, wv, wo, u0, u1, dA, dB, vec, q, k, v, ctx, lse, mid, act, dg,
             dx, dxb, gmix, gout, gup, gdown, gvec, gbup, dh, gm, ga, cbuf, dctx, dm, dkT, dvT, stage, ssem, ready=lambda n: None):
    gvec[...]=jnp.zeros_like(gvec); gbup[...]=jnp.zeros_like(gbup)
    def cs(t): return jnp.sum(t,0,keepdims=True)
    def st1(i,_):
        r=rows_of(i)
        gb=g[r,:]; gf=gb.astype(f32)
        dc=jnp.zeros((RB,D),f32)
        for j in range(FF//FB):
            cc=slice(j*FB,(j+1)*FB)
            d=((nt(gb[:,0:512],flat(dA,j))+nt(gb[:,512:],flat(dB,j)))*dg[r,cc].astype(f32)).astype(bf16)
            dh[r,cc]=d
            gbup[0:1,cc]+=cs(d.astype(f32))
            dc=dc+nt(d,cols((u0,u1)[j//2],(j%2)*FB,FB))
        xh,rstd=norm_parts(mid[r,:])
        cbuf[r,:]=(xh*vec[5:6,:]+vec[6:7,:]).astype(bf16)
        e=dc*vec[5:6,:]
        gmv=gf+(e-jnp.mean(e,-1,keepdims=True)-xh*jnp.mean(e*xh,-1,keepdims=True))*rstd
        gm[r,:]=gmv
        gav=gmv.astype(bf16); ga[r,:]=gav
        gvec[4:5,:]+=cs(gav.astype(f32)); gvec[5:6,:]+=cs(dc*xh); gvec[6:7,:]+=cs(dc); gvec[7:8,:]+=cs(gf)
        dctx[r,:]=nt(gav,flat(wo)).astype(bf16)
        return 0
    lax.fori_loop(0,NB,st1,0)
    for n in ('q','k','v','lse'): ready(n)
    kb=jnp.where(lax.broadcasted_iota(jnp.int32,(1,LEN),1)<length,0.0,-1e30).astype(f32)
    tri=lax.broadcasted_iota(jnp.int32,(RB,RB),1)<=lax.broadcasted_iota(jnp.int32,(RB,RB),0)
    lane=lax.broadcasted_iota(jnp.int32,(RB,128),1)
    lanek=lax.broadcasted_iota(jnp.int32,(LEN,128),1)
    def att(p,_):
        c=pl.ds(pl.multiple_of(p*128,128),128)
        dkT[...]=jnp.zeros_like(dkT); dvT[...]=jnp.zeros_like(dvT)
        for i in range(NB):
            lo=i*RB; r=slice(lo,lo+RB)
            qp=q[r,c]; dcp=dctx[r,c]; lr=lse[r,:]
            qT=qp.astype(f32).T.astype(bf16); dcT=dcp.astype(f32).T.astype(bf16)
            dq=None
            for h in range(2):
                sel=(lane<64)==(h==0)
                qh=jnp.where(sel,qp,jnp.zeros_like(qp)); dch=jnp.where(sel,dcp,jnp.zeros_like(dcp))
                ls=jnp.sum(jnp.where(lane==2*p+h,lr,0.0),-1,keepdims=True)
                hs=slice(h*64,h*64+64)
                pd=jnp.exp(jnp.where(tri,nt(qh,k[r,c])+kb[:,lo:lo+RB],-1e30)-ls)
                dpd=nt(dch,v[r,c])
                delta=jnp.sum(pd*dpd,-1,keepdims=True)
                if i:
                    plft=jnp.exp(nt(qh,k[0:lo,c])+kb[:,0:lo]-ls)
                    dpl=nt(dch,v[0:lo,c])
                    delta=delta+jnp.sum(plft*dpl,-1,keepdims=True)
                dsd=(pd*(dpd-delta)).astype(bf16)
                dkT[hs,r]+=nn(qT[hs],dsd); dvT[hs,r]+=nn(dcT[hs],pd.astype(bf16))
                t=nn(dsd,k[r,c])
                if i:
                    dsl=(plft*(dpl-delta)).astype(bf16)
                    dkT[hs,0:lo]+=nn(qT[hs],dsl); dvT[hs,0:lo]+=nn(dcT[hs],plft.astype(bf16))
                    t=t+nn(dsl,k[0:lo,c])
                dq=t if h==0 else jnp.where(lane<64,dq,t)
            dm[r,c]=(dq*0.125).astype(bf16)
        dm[:,pl.ds(pl.multiple_of(D+p*128,128),128)]=dkT[...].T.astype(bf16)
        dm[:,pl.ds(pl.multiple_of(2*D+p*128,128),128)]=dvT[...].T.astype(bf16)
        return 0
    lax.fori_loop(0,D//128,att,0)
    def put(n,dst,val):
        slot=n%2
        def cp(): return pltpu.make_async_copy(stage.at[slot],dst,ssem.at[slot])
        @pl.when(n>=2)
        def _(): cp().wait()
        stage[slot]=val
        cp().start()
    ready("act")
    def gd(m,_):
        rr=rows_of(m)
        put(m,gdown.at[rr,:],tn(act[:,rr],g[...]).astype(bf16)); return 0
    lax.fori_loop(0,FF//RB,gd,0)
    def gu(m,_):
        rr=rows_of(m)
        for j in range(FF//FB):
            cc=slice(j*FB,(j+1)*FB)
            put(12+4*m+j,gup.at[rr,cc],tn(cbuf[:,rr],dh[:,cc]).astype(bf16))
        return 0
    lax.fori_loop(0,D//RB,gu,0)
    ready("ctx")
    for t in range(3):
        rr=slice(t*256,t*256+256)
        put(24+t,gout.at[rr,:],tn(ctx[:,rr],ga[...]).astype(bf16))
    for n in ("x","wq","wk","wv"): ready(n)
    def st3(i,_):
        r=rows_of(i)
        d=dm[r,:]; df=d.astype(f32)
        gvec[2:3,:]+=cs(df[:,0:D]); gvec[3:4,:]+=cs(df[:,2*D:])
        da=nt(d[:,0:D],flat(wq))+nt(d[:,D:2*D],flat(wk))+nt(d[:,2*D:],flat(wv))
        xh,rstd=norm_parts(x[r,:].astype(f32))
        cbuf[r,:]=(xh*vec[0:1,:]+vec[1:2,:]).astype(bf16)
        gvec[0:1,:]+=cs(da*xh); gvec[1:2,:]+=cs(da)
        e=da*vec[0:1,:]
        o=gm[r,:]+(e-jnp.mean(e,-1,keepdims=True)-xh*jnp.mean(e*xh,-1,keepdims=True))*rstd
        dx[r,:]=o; dxb[r,:]=o.astype(bf16)
        return 0
    lax.fori_loop(0,NB,st3,0)
    def gmx(m,_):
        rr=rows_of(m)
        for j in range(3):
            cc=slice(j*D,(j+1)*D)
            put(27+3*m+j,gmix.at[rr,cc],tn(cbuf[:,rr],dm[:,cc]).astype(bf16))
        return 0
    lax.fori_loop(0,D//RB,gmx,0)
    for n in (34,35): pltpu.make_async_copy(stage.at[n%2],gmix.at[rows_of(2),0:D],ssem.at[n%2]).wait()

VM = pl.BlockSpec(memory_space=pltpu.VMEM)
SM = pl.BlockSpec(memory_space=pltpu.SMEM)
AN = pl.BlockSpec(memory_space=pl.ANY)
MESH = pl.DeviceIdType.MESH
MIB = 2**20
STEP = 10
TABLE = 8 + FF // D


def S(shape, dtype):
    return jax.ShapeDtypeStruct(shape, dtype)


def vm_like(items):
    return [pltpu.VMEM(i.shape, i.dtype) for i in items]


def flat(ref, z=None):
    w = ref[...] if z is None else ref[z]
    return w.reshape(-1, w.shape[-1])


def cols(ref, lo, n):
    w = ref[:, :, :, :, lo : lo + n]
    return w.reshape(-1, n)


ZS, YS, XS = 4, 2, 2


def place():
    s = lax.axis_index("section")
    d = lax.axis_index("dp")
    return s, d // (YS * XS), (d // XS) % YS, d % XS


def at_chip(s, z, y, x):
    return (s, z * (YS * XS) + y * XS + x)


def partners(s, z, y, x):
    others = [at_chip(1 - s, z, y, x), at_chip(s, z, y, 1 - x), at_chip(s, z, 1 - y, x)]
    return others + [at_chip(s, (z + r) % ZS, y, x) for r in range(1, ZS)]


def greet(devices):
    barrier = pltpu.get_barrier_semaphore()
    for dev in devices:
        pl.semaphore_signal(barrier, inc=1, device_id=dev, device_id_type=MESH)
    pl.semaphore_wait(barrier, len(devices))


CHUNKS = ("vec", "wq", "wk", "wv", "wo", "u0", "u1", "dA", "dB")
NC = len(CHUNKS)
VL = 384


def mask_table(j):
    row = lax.broadcasted_iota(jnp.int32, (48, VL), 0)
    lane = lax.broadcasted_iota(jnp.int32, (48, VL), 1)
    one = [lane == 48 * (j % 8) + row] + [lane == 192 * (j % 2) + 4 * row + t for t in range(4)]
    return [m.astype(f32).astype(bf16) for m in one]


def front(lengths, inputs, masters, vec48):
    chunk = [(16, VL)] + [(48, D)] * 4 + [(48, FF // 2)] * 2 + [(192, 512), (192, 256)]
    saved = [S((LEN, D), bf16)] * 5 + [S((LEN, 128), f32), S((LEN, D), f32), S((LEN, FF), bf16), S((LEN, FF), bf16)]
    half = ZS // 2

    def kern(len_ref, x_h, mix, out, up, down, v48, *refs):
        full, refs = refs[:NC], refs[NC:]
        tabs, refs = refs[:2], refs[2:]
        keep, refs = (refs[:9], refs[9:18]), refs[18:]
        own, refs = refs[:NC], refs[NC:]
        wv, refs = refs[:NC], refs[NC:]
        x0, y0, y1, ab, q, k, v, ctx, lse, mid, act, dg, bup, send, recv, loc, lsem, ksem = refs
        s, z, y, x = place()
        length = len_ref[s]
        near = partners(s, z, y, x)
        sib, px, py, pz = near[0], near[1], near[2], near[3:]
        x_in = pltpu.make_async_copy(x_h.at[s], x0, lsem.at[NC])
        x_in.start()
        greet(near)
        lo, hi = slice(0, half), slice(half, ZS)

        def copy(a, slot, idx, dev, source=None):
            dst = full[a].at[idx]
            return pltpu.make_async_remote_copy(
                src_ref=dst if source is None else source, dst_ref=dst, send_sem=send.at[a, slot],
                recv_sem=recv.at[a, slot], device_id=dev, device_id_type=MESH)

        def local(a):
            return pltpu.make_async_copy(own[a], full[a].at[s, z, y, x], loc.at[a])

        def prepare(a):
            if a == 0:
                maps = mask_table((z * YS + y) * XS + x)
                vb = v48[...].astype(bf16)
                own[0][...] = jnp.zeros_like(own[0])
                own[0][0:8, :] = tn(vb, maps[0])[0:8].astype(bf16)
                ups = sum(tn(vb, maps[1 + t])[8 + t : 9 + t] for t in range(4))
                own[0][8:16, :] = jnp.broadcast_to(ups, (8, VL)).astype(bf16)
            elif a < 4:
                own[a][...] = mix[:, (a - 1) * D : a * D].astype(bf16)
            elif a == 4:
                own[a][...] = out[...].astype(bf16)
            elif a < 7:
                own[a][...] = up[:, (a - 5) * (FF // 2) : (a - 4) * (FF // 2)].astype(bf16)
            else:
                own[a][...] = (down[:, 0:512] if a == 7 else down[:, 512:D]).astype(bf16)

        def first(a):
            local(a).start()
            for r in range(1, ZS):
                copy(a, r - 1, (s, z, y, x), pz[r - 1], own[a]).start()

        second_out = [(3, (s, lo, y, x), px), (4, (s, hi, y, x), py)]
        second_in = [(3, (s, lo, y, 1 - x), px), (4, (s, hi, 1 - y, x), py)]
        third_out = [(5, (s, lo, y), py), (6, (s, hi, slice(None), x), px)]
        third_in = [(5, (s, lo, 1 - y), py), (6, (s, hi, slice(None), 1 - x), px)]

        def waves(l):
            return [
                [(7, (l, slice(None), y, x), sib)],
                [(8, (l, lo, y, 1 - x), sib), (9, (l, hi, 1 - y, x), sib)],
                [(10, (l, lo, 1 - y), sib), (11, (l, hi, slice(None), 1 - x), sib)],
            ]

        def second(a):
            for r in range(1, ZS):
                copy(a, r - 1, (s, (z - r) % ZS, y, x), pz[r - 1]).wait_recv()
            local(a).wait()
            for c in second_out + waves(s)[0]:
                copy(a, *c).start()

        def third(a):
            for c in second_in:
                copy(a, *c).wait_recv()
            for c in third_out + waves(s)[1]:
                copy(a, *c).start()

        def last(a):
            for c in third_in:
                copy(a, *c).wait_recv()
            for c in waves(s)[2]:
                copy(a, *c).start()

        seen = set()

        def event(l, *what):
            todo = [w for w in what if (l, w) not in seen and w[1] < NC]
            seen.update((l, w) for w in todo)
            if todo:
                @pl.when(s == l)
                def _():
                    for stage, a in todo:
                        stage(a)

        def group(l, a):
            event(l, (third, a), (second, a + 2))

        def load(l, a):
            return pltpu.make_async_copy(full[a].at[l], wv[a], lsem.at[a])

        def complete(l, a):
            event(l, (last, a))

            @pl.when(s != l)
            def _():
                for wave in waves(l):
                    for c in wave:
                        copy(a, *c).wait_recv()
            load(l, a).start()
            load(l, a).wait()

        def store(l, i):
            return pltpu.make_async_copy((None, q, k, v, ctx, lse, mid, act, dg)[i] if i else (y0, y1)[l], keep[l][i], ksem.at[i])

        kb = jnp.where(lax.broadcasted_iota(jnp.int32, (1, LEN), 1) < length, 0.0, -1e30).astype(f32)
        tri = lax.broadcasted_iota(jnp.int32, (RB, RB), 1) <= lax.broadcasted_iota(jnp.int32, (RB, RB), 0)
        lane = lax.broadcasted_iota(jnp.int32, (RB, 128), 1)

        def layer(l, xin, yout):
            vec = tabs[l]

            def settle(i):
                if l:
                    store(0, i).wait()

            complete(l, 0)
            pv = wv[0][...].reshape(16, 16, VL).astype(f32)
            vec[:, 0:VL] = sum(pv[j, 0:8] for j in range(8))
            vec[:, VL:D] = sum(pv[j, 0:8] for j in range(8, 16))
            for m in range(8):
                bup[:, m * VL : (m + 1) * VL] = pv[2 * m, 8:16] + pv[2 * m + 1, 8:16]

            def norm1(i, _):
                r = rows_of(i)
                xh, _r = norm_parts(xin[r, :].astype(f32))
                ab[r, :] = (xh * vec[0:1, :] + vec[1:2, :]).astype(bf16)
                return 0

            lax.fori_loop(0, NB, norm1, 0)

            def project(a, dst, f):
                def step(i, _):
                    r = rows_of(i)
                    dst[r, :] = f(nn(ab[r, :], flat(wv[a]))).astype(bf16)
                    return 0

                lax.fori_loop(0, NB, step, 0)

            complete(l, 1)
            group(l, 3)
            settle(1)
            project(1, q, lambda t: (t + vec[2:3, :]).astype(bf16).astype(f32) * 0.125)
            store(l, 1).start()
            complete(l, 2)
            group(l, 4)
            settle(2)
            project(2, k, lambda t: t)
            store(l, 2).start()
            complete(l, 3)
            group(l, 5)
            settle(3)
            project(3, v, lambda t: t + vec[3:4, :])
            store(l, 3).start()
            settle(4)
            settle(5)
            lse[...] = jnp.zeros_like(lse)

            def att(p, _):
                @pl.when(p == 1)
                def _():
                    group(l, 6)

                @pl.when(p == 2)
                def _():
                    event(l, (last, 4))

                @pl.when(p == 5)
                def _():
                    group(l, 7)
                    event(l, (last, 5))

                c = pl.ds(pl.multiple_of(p * 128, 128), 128)
                for i in range(NB):
                    top = i * RB
                    r = slice(top, top + RB)
                    qp = q[r, c]
                    outs = []
                    ls = []
                    for h in range(2):
                        qh = jnp.where((lane < 64) == (h == 0), qp, jnp.zeros_like(qp))
                        sd = jnp.where(tri, nt(qh, k[r, c]) + kb[:, top : top + RB], -1e30)
                        m = jnp.max(sd, -1, keepdims=True)
                        if i:
                            sl = nt(qh, k[0:top, c]) + kb[:, 0:top]
                            m = jnp.maximum(m, jnp.max(sl, -1, keepdims=True))
                        ed = jnp.exp(sd - m)
                        tot = jnp.sum(ed, -1, keepdims=True)
                        o = nn(ed.astype(bf16), v[r, c])
                        if i:
                            el = jnp.exp(sl - m)
                            tot = tot + jnp.sum(el, -1, keepdims=True)
                            o = o + nn(el.astype(bf16), v[0:top, c])
                        outs.append(o * (1.0 / tot))
                        ls.append(m + jnp.log(tot))
                    ctx[r, c] = jnp.where(lane < 64, outs[0], outs[1]).astype(bf16)
                    lse[r, :] = jnp.where(lane == 2 * p, ls[0], jnp.where(lane == 2 * p + 1, ls[1], lse[r, :]))
                return 0

            lax.fori_loop(0, D // 128, att, 0)
            store(l, 4).start()
            store(l, 5).start()
            if l == 0:
                event(1, *[(first, a) for a in range(NC)])
            complete(l, 4)
            settle(6)

            def middle(i, _):
                r = rows_of(i)
                md = xin[r, :].astype(f32) + nn(ctx[r, :], flat(wv[4])) + vec[4:5, :]
                mid[r, :] = md
                xh, _r = norm_parts(md)
                ab[r, :] = (xh * vec[5:6, :] + vec[6:7, :]).astype(bf16)
                return 0

            lax.fori_loop(0, NB, middle, 0)
            store(l, 6).start()
            settle(7)
            settle(8)
            for a in (5, 6):
                complete(l, a)
                if a == 5:
                    group(l, 8)

                def expand(i, _):
                    r = rows_of(i)
                    for j in range(2):
                        off = (a - 5) * (FF // 2) + j * FB
                        cc = slice(off, off + FB)
                        h = nn(ab[r, :], cols(wv[a], j * FB, FB)) + bup[0:1, cc]
                        h2 = h * h
                        t = jnp.tanh(h * (K0 + (K0 * K1) * h2))
                        hf = 0.5 + 0.5 * t
                        act[r, cc] = (h * hf).astype(bf16)
                        dg[r, cc] = (hf + (0.5 * h) * (1.0 - t * t) * (K0 + (3 * K0 * K1) * h2)).astype(bf16)
                    return 0

                lax.fori_loop(0, NB, expand, 0)
            store(l, 7).start()
            store(l, 8).start()
            if l == 0:
                event(1, (second, 0), (second, 1), (second, 2))
            for a, lo_, hi_ in ((7, 0, 512), (8, 512, D)):
                complete(l, a)
                if l == 0:
                    event(1, *([(third, 0), (third, 1), (second, 3)] if a == 7 else [(third, 2), (second, 4)]))

                def contract(i, _):
                    r = rows_of(i)
                    t = mid[r, lo_:hi_] + nn(act[r, :], flat(wv[a])) + vec[7:8, lo_:hi_]
                    yout[r, lo_:hi_] = t.astype(bf16)
                    return 0

                lax.fori_loop(0, NB, contract, 0)
            store(l, 0).start()

        for a in range(NC):
            prepare(a)
            event(0, (first, a))
        event(0, (second, 0), (second, 1), (second, 2), (third, 0), (third, 1), (second, 3), (third, 2), (second, 4))
        x_in.wait()
        layer(0, x0, y0)
        layer(1, y0, y1)
        store(0, 0).wait()
        for i in range(9):
            store(1, i).wait()
        for a in range(NC):
            for r in range(1, ZS):
                copy(a, r - 1, (s, z, y, x), pz[r - 1], own[a]).wait_send()
            for c in second_out + third_out + sum(waves(s), []):
                copy(a, *c).wait_send()

    outs = [S((2, ZS, YS, XS) + c, bf16) for c in chunk] + [S((8, D), f32)] * 2 + saved * 2
    act_ = [S((LEN, D), bf16)] * 4 + saved[1:] + [S((8, FF), f32)]
    return pl.pallas_call(
        kern,
        out_shape=outs,
        in_specs=[SM, AN] + [VM] * 5,
        out_specs=[AN] * NC + [VM] * 2 + [AN] * 18,
        scratch_shapes=vm_like([S(c, bf16) for c in chunk] + [S((ZS, YS, XS) + c, bf16) for c in chunk] + act_)
        + [pltpu.SemaphoreType.DMA((NC, 12)), pltpu.SemaphoreType.DMA((NC, 12)), pltpu.SemaphoreType.DMA((NC,)), pltpu.SemaphoreType.DMA((NC + 1,)), pltpu.SemaphoreType.DMA((9,))],
        compiler_params=pltpu.CompilerParams(collective_id=1, has_side_effects=True, vmem_limit_bytes=60 * MIB),
        name="front",
    )(lengths, inputs, *masters, vec48)


def layer_bwd(layer, length, g, x, weights, table, saved):
    names = ["g", "dg", "dA", "dB", "u0", "u1", "mid", "wo", "q", "k", "v", "lse", "act", "ctx", "x", "wq", "wk", "wv"]
    q, k, v, ctx, lse, mid, act, dg = saved
    wn = CHUNKS[1:]
    vals = dict(g=g, dg=dg, mid=mid, q=q, k=k, v=v, lse=lse, act=act, ctx=ctx, x=x, **dict(zip(wn, weights)))
    arrs = [vals[n] for n in names]
    hold = [S(vals[n].shape[1:] if n in wn else vals[n].shape, vals[n].dtype) for n in names]

    def kern(l, vec, *refs):
        n = len(names)
        hb = dict(zip(names, refs[:n]))
        outs = refs[n : n + 8]
        refs = refs[n + 8 :]
        vm = dict(zip(names, refs[:n]))
        lsem, scr = refs[n], refs[n + 1 :]
        cps = {
            nm: pltpu.make_async_copy(hb[nm].at[layer] if nm in wn else hb[nm], vm[nm], lsem.at[i])
            for i, nm in enumerate(names)
        }
        for nm in names:
            cps[nm].start()

        def ready(nm):
            cps[nm].wait()

        for nm in names[:8]:
            ready(nm)
        bwd_body(
            l[0], vm["g"], vm["x"], *[vm[n] for n in wn], vec,
            vm["q"], vm["k"], vm["v"], vm["ctx"], vm["lse"], vm["mid"], vm["act"], vm["dg"],
            *outs, vm["dg"], *scr, ready=ready,
        )

    return pl.pallas_call(
        kern,
        out_shape=[S((LEN, D), f32), S((LEN, D), bf16), S((D, 3 * D), bf16), S((D, D), bf16), S((D, FF), bf16), S((FF, D), bf16), S((8, D), f32), S((8, FF), f32)],
        in_specs=[SM, VM] + [AN] * 18,
        out_specs=[VM] * 2 + [AN] * 4 + [VM] * 2,
        scratch_shapes=vm_like(hold) + [pltpu.SemaphoreType.DMA((18,))]
        + vm_like([S((LEN, D), f32)] + [S((LEN, D), bf16)] * 3 + [S((LEN, 3 * D), bf16)] + [S((128, LEN), f32)] * 2 + [S((2, RB, D), bf16)])
        + [pltpu.SemaphoreType.DMA((2,))],
        compiler_params=pltpu.CompilerParams(vmem_limit_bytes=63 * MIB),
        name="layer_bwd",
    )(length, table, *arrs)


def scatter_grads(grads0, grads1):
    n = len(grads0)
    half = ZS // 2
    blocks = [g.shape[3:] for g in grads0]

    def kern(*refs):
        g0, g1 = refs[:n], refs[n : 2 * n]
        outs, total = refs[2 * n : 3 * n], refs[3 * n]
        refs = refs[3 * n + 1 :]
        own, sibs, a2, b2, a3, b3, r4 = [refs[i * n : (i + 1) * n] for i in range(7)]
        norms, send, recv, loc, nsend, nrecv = refs[7 * n :]
        s, z, y, x = place()
        near = partners(s, z, y, x)
        sib, px, py, pz = near[0], near[1], near[2], near[3:]
        greet(near)
        lo, hi = slice(0, half), slice(half, ZS)

        def copy(a, slot, src, dst, dev):
            return pltpu.make_async_remote_copy(
                src_ref=src, dst_ref=dst, send_sem=send.at[a, slot], recv_sem=recv.at[a, slot],
                device_id=dev, device_id_type=MESH)

        def to_sib(a, src):
            return copy(a, 0, src[a], sibs[a], sib)

        def local(a, src):
            return pltpu.make_async_copy(src[a], own[a], loc.at[a])

        for core, mine, other in ((0, g0, g1), (1, g1, g0)):
            @pl.when(s == core)
            def _():
                for a in range(n):
                    local(a, mine).start()
                    to_sib(a, other).start()

        def add(ref, idx, other, oidx):
            ref[idx] = (ref[idx].astype(f32) + other[oidx].astype(f32)).astype(ref.dtype)

        def second(a):
            return [copy(a, 1, own[a].at[lo, 1 - y], a2[a], py), copy(a, 2, own[a].at[hi, :, 1 - x], b2[a], px)]

        def third(a):
            return [copy(a, 3, own[a].at[lo, y, 1 - x], a3[a], px), copy(a, 4, own[a].at[hi, 1 - y, x], b3[a], py)]

        def fourth(a):
            return [copy(a, 4 + r, own[a].at[(z + r) % ZS, y, x], r4[a].at[r - 1], pz[r - 1]) for r in range(1, ZS)]

        def one(a):
            local(a, g0).wait()
            to_sib(a, g0).wait_recv()

            def step(i, _):
                idx = (i // (YS * XS), (i // XS) % YS, i % XS)
                add(own[a], idx, sibs[a], idx)
                return 0

            lax.fori_loop(0, ZS * YS * XS, step, 0)
            for c in second(a):
                c.start()

        def two(a):
            for c in second(a):
                c.wait()

            def step(i, _):
                h, j = i // 2, i % 2
                add(own[a], (h, y, j), a2[a], (h, j))
                add(own[a], (half + h, j, x), b2[a], (h, j))
                return 0

            lax.fori_loop(0, half * 2, step, 0)
            for c in third(a):
                c.start()

        def three(a):
            for c in third(a):
                c.wait()

            def step(h, _):
                add(own[a], (h, y, x), a3[a], (h,))
                add(own[a], (half + h, y, x), b3[a], (h,))
                return 0

            lax.fori_loop(0, half, step, 0)
            for c in fourth(a):
                c.start()

        def four(a):
            for c in fourth(a):
                c.wait()
            v = own[a][z, y, x].astype(f32)
            for r in range(ZS - 1):
                v = v + r4[a][r].astype(f32)
            outs[a][...] = v
            return jnp.sum(v * v)

        square = jnp.zeros((), f32)
        stages = (one, two, three, four)
        for t in range(n + 3):
            for k, stage in enumerate(stages):
                if 0 <= t - k < n:
                    got = stage(t - k)
                    if k == 3:
                        square = square + got
        for a in range(n):
            to_sib(a, g0).wait_send()

        def shared(k, dev, slot):
            return pltpu.make_async_remote_copy(
                src_ref=norms.at[k], dst_ref=norms.at[slot], send_sem=nsend.at[slot], recv_sem=nrecv.at[slot],
                device_id=dev, device_id_type=MESH)

        norms[0] = jnp.zeros((8, 128), f32) + square
        for k, dev in enumerate((sib, px, py)):
            c = shared(2 * k, dev, 2 * k + 1)
            c.start()
            c.wait()
            norms[2 * k + 2] = norms[2 * k] + norms[2 * k + 1]
        cs = [shared(6, pz[r], 7 + r) for r in range(ZS - 1)]
        for c in cs:
            c.start()
        for c in cs:
            c.wait()
        total[...] = norms[6] + norms[7] + norms[8] + norms[9]

    def buf(lead, a):
        return pltpu.VMEM(lead + blocks[a], grads0[a].dtype)

    scratch = []
    for lead in ((ZS, YS, XS), (ZS, YS, XS), (half, XS), (half, YS), (half,), (half,), (ZS - 1,)):
        scratch += [buf(lead, a) for a in range(n)]
    return pl.pallas_call(
        kern,
        out_shape=[S(b, f32) for b in blocks] + [S((8, 128), f32)],
        in_specs=[AN] * (2 * n),
        out_specs=[VM] * (n + 1),
        scratch_shapes=scratch
        + [pltpu.VMEM((10, 8, 128), f32), pltpu.SemaphoreType.DMA((n, 8)), pltpu.SemaphoreType.DMA((n, 8)), pltpu.SemaphoreType.DMA((n,)),
           pltpu.SemaphoreType.DMA((10,)), pltpu.SemaphoreType.DMA((10,))],
        compiler_params=pltpu.CompilerParams(collective_id=2, has_side_effects=True, vmem_limit_bytes=60 * MIB),
        name="scatter_grads",
    )(*grads0, *grads1)


RATES = (0.05, 0.25, 0.05, 0.05, 0.5)
DECAYS = (0.1, 0.1, 0.1, 0.1, 0.0)


def adam(total, grads, masters, firsts, seconds):
    n = len(grads)
    flat = [a for four in zip(grads, masters, firsts, seconds) for a in four]
    steps = 6

    def spec(a):
        if a.shape[0] % (8 * steps):
            return pl.BlockSpec(a.shape, lambda i: (0, 0))
        return pl.BlockSpec((a.shape[0] // steps, a.shape[1]), lambda i: (i, 0))

    def kern(t, *refs):
        norm = jnp.sqrt(t[0:1, 0:1])
        factor = jnp.minimum(1.0, 1.0 / (norm + 1e-06))
        for i in range(n):
            gr, w, m, u = (r[...] for r in refs[4 * i : 4 * i + 4])
            mo, uo, wo = refs[4 * n + 3 * i : 4 * n + 3 * i + 3]
            gr = gr * factor
            m1 = 0.9 * m + (1.0 - 0.9) * gr
            u1 = 0.999 * u + (1.0 - 0.999) * gr * gr
            mh = m1 / (1.0 - 0.9**STEP)
            uh = u1 / (1.0 - 0.999**STEP)
            mo[...] = m1
            uo[...] = u1
            wo[...] = w - RATES[i] * (mh / (jnp.sqrt(uh) + 1e-08) + DECAYS[i] * w)

    outs = [S(a.shape, f32) for a in masters for _ in range(3)]
    return pl.pallas_call(
        kern,
        grid=(steps,),
        out_shape=outs,
        in_specs=[pl.BlockSpec((8, 128), lambda i: (0, 0))] + [spec(a) for a in flat],
        out_specs=[spec(a) for a in outs],
        compiler_params=pltpu.CompilerParams(vmem_limit_bytes=32 * MIB),
        name="adam",
    )(total, *flat)


def swap(v):
    return lax.ppermute(v, "section", [(0, 1), (1, 0)])


def plain_fwd(x, length, weights, vec, bup):
    mix, out, up, down = weights
    row = lambda i: vec[i][None]
    xf = x.astype(f32)
    a = (norm_parts(xf)[0] * row(0) + row(1)).astype(bf16)
    m = nn(a, mix)
    q = ((m[:, :D] + row(2)).astype(bf16).astype(f32) * 0.125).astype(bf16)
    k = m[:, D : 2 * D].astype(bf16)
    v = (m[:, 2 * D :] + row(3)).astype(bf16)
    heads = [t.reshape(LEN, D // 64, 64) for t in (q, k, v)]
    sc = jnp.einsum("qhe,khe->hqk", heads[0], heads[1], preferred_element_type=f32)
    pos = jnp.arange(LEN)
    sc = jnp.where(((pos[None, :] <= pos[:, None]) & (pos[None, :] < length[0]))[None], sc, -1e30)
    top = jnp.max(sc, -1, keepdims=True)
    e = jnp.exp(sc - top)
    tot = jnp.sum(e, -1, keepdims=True)
    ctx = jnp.einsum("hqk,khe->qhe", (e / tot).astype(bf16), heads[2], preferred_element_type=f32).reshape(LEN, D).astype(bf16)
    lse = jnp.pad((top + jnp.log(tot))[:, :, 0].T, ((0, 0), (0, 128 - D // 64)))
    mid = xf + nn(ctx, out) + row(4)
    c = (norm_parts(mid)[0] * row(5) + row(6)).astype(bf16)
    h = nn(c, up) + bup
    t = jnp.tanh(h * (K0 + (K0 * K1) * h * h))
    hf = 0.5 + 0.5 * t
    act = (h * hf).astype(bf16)
    dg = (hf + (0.5 * h) * (1.0 - t * t) * (K0 + (3 * K0 * K1) * h * h)).astype(bf16)
    y = (mid + nn(act, down) + row(7)).astype(bf16)
    return y, q, k, v, ctx, lse, mid, act, dg


def on_device(inputs, cotangent, lengths, mix, out, up, down, vectors, *moments):
    s = lax.axis_index("section")
    n_dp = lax.axis_size("dp")
    custom = n_dp == ZS * YS * XS
    masters = [m[0] for m in (mix, out, up, down)] + [vectors]
    firsts = [m[0] for m in moments[:4]] + [moments[4]]
    seconds = [m[0] for m in moments[5:9]] + [moments[9]]
    part = vectors.shape[1]
    length = lax.dynamic_slice_in_dim(lengths, s, 1)
    x0 = lax.dynamic_index_in_dim(inputs, s, 0, keepdims=False)
    cot = lax.dynamic_index_in_dim(cotangent, s, 0, keepdims=False)
    g1 = jnp.where(jnp.arange(LEN, dtype=jnp.int32)[:, None] < length[0], cot, jnp.zeros_like(cot))
    if custom:
        got = front(lengths, inputs, masters[:4], vectors.reshape(48, TABLE))
        weights, tables, (passed, *saved0), (final, *saved1) = got[1:NC], got[NC : NC + 2], got[NC + 2 : NC + 11], got[NC + 11 :]
    else:
        full = [lax.all_gather(m.astype(bf16), "dp", axis=0, tiled=True) for m in masters[:4]]
        full.append(lax.all_gather(vectors[0].astype(bf16), "dp", axis=0, tiled=True))
        full = [jnp.where(s == 0, jnp.stack([w, o]), jnp.stack([o, w])) for w, o in ((w, swap(w)) for w in full)]
        slots = full[4].astype(f32).reshape(2, D, TABLE)
        tables = slots[:, :, :8].transpose(0, 2, 1)
        bups = slots[:, :, 8:].reshape(2, 1, FF)
        mix_, out_, up_, down_ = full[:4]
        weights = [mix_[:, :, :D], mix_[:, :, D : 2 * D], mix_[:, :, 2 * D :], out_, up_[:, :, : FF // 2], up_[:, :, FF // 2 :], down_[:, :, :512], down_[:, :, 512:]]
        weights = [w.reshape(2, ZS, YS, XS, -1, w.shape[-1]) for w in weights]
        passed, *saved0 = plain_fwd(x0, length, [w[0] for w in full[:4]], tables[0], bups[0])
        final, *saved1 = plain_fwd(passed, length, [w[1] for w in full[:4]], tables[1], bups[1])
    other = swap(jnp.where(s == 0, final, passed))
    activations = jnp.where(s == 0, jnp.stack([passed, other]), jnp.stack([other, final]))[None]
    dx1, g0, *grads1 = layer_bwd(1, length, g1, passed, weights, tables[1], saved1)
    dx0, _, *grads0 = layer_bwd(0, length, g0, x0, weights, tables[0], saved0)
    other = swap(jnp.where(s == 0, dx1, dx0))
    input_grads = jnp.where(s == 0, jnp.stack([dx0, other]), jnp.stack([other, dx1]))[None]

    def vector_grads(gvec, gbup):
        return jnp.concatenate([gvec.T, gbup[0].reshape(D, FF // D)], 1).reshape(-1)

    vec_grads = [vector_grads(*g[4:]) for g in (grads0, grads1)]
    if custom:
        packed = [
            [g.reshape(ZS, YS, XS, -1, g.shape[-1]) for g in gs[:4]]
            + [jnp.pad(v.reshape(n_dp, part), ((0, 0), (0, 1024 - part))).reshape(ZS, YS, XS, 8, 128)]
            for gs, v in ((grads0, vec_grads[0]), (grads1, vec_grads[1]))
        ]
        *shards, total = scatter_grads(*packed)
        shards[4] = shards[4].reshape(1, 1024)[:, :part]
    else:
        shards = []
        for g0_, g1_ in list(zip(grads0[:4], grads1[:4])) + [tuple(vec_grads)]:
            g0_, g1_ = g0_.astype(f32), g1_.astype(f32)
            both = jnp.where(s == 0, g0_, g1_) + swap(jnp.where(s == 0, g1_, g0_))
            shards.append(lax.psum_scatter(both, "dp", scatter_dimension=0, tiled=True))
        shards[4] = shards[4][None]
        total = jnp.full((8, 128), lax.psum(sum(jnp.sum(g * g) for g in shards), ("section", "dp")))
    results = adam(total, shards, masters, firsts, seconds)
    results = [r if i >= 12 else r[None] for i, r in enumerate(results)]
    return (activations, input_grads, jnp.sqrt(total[0, 0])) + tuple(results)


def solution(mesh):
    rows = P("dp", None, None)
    mats = (P("section", "dp", None),) * 4
    vec = (P("section", "dp"),)
    acts = P("section", "dp", None, None)
    return jax.shard_map(
        on_device,
        mesh=mesh,
        in_specs=(rows, rows, P("dp")) + (mats + vec) * 3,
        out_specs=(acts, acts, P()) + (P("section", "dp", None),) * 12 + vec * 3,
        check_vma=False,
    )
```

```python
import jax, jax.numpy as jnp
from jax import lax
from jax.experimental import pallas as pl
from jax.experimental.pallas import tpu as pltpu
from jax.sharding import PartitionSpec as P
D=768; FF=3072; LEN=1024; RB=256; NB=LEN//RB; FB=768
f32=jnp.float32; bf16=jnp.bfloat16
NT=(((1,),(1,)),((),())); TN=(((0,),(0,)),((),()))
def nn(a,b): return jnp.dot(a,b,preferred_element_type=f32)
def nt(a,b): return lax.dot_general(a,b,NT,preferred_element_type=f32)
def tn(a,b): return lax.dot_general(a,b,TN,preferred_element_type=f32)
K0=0.7978845608028654; K1=0.044715
def rows_of(i): return pl.ds(pl.multiple_of(i*RB,RB),RB)
def norm_parts(v):
    cen=v-jnp.mean(v,-1,keepdims=True)
    rstd=lax.rsqrt(jnp.mean(cen*cen,-1,keepdims=True)+1e-5)
    return cen*rstd, rstd
VM = pl.BlockSpec(memory_space=pltpu.VMEM)
SM = pl.BlockSpec(memory_space=pltpu.SMEM)
AN = pl.BlockSpec(memory_space=pl.ANY)
MESH = pl.DeviceIdType.MESH
MIB = 2**20
STEP = 10
TABLE = 8 + FF // D


def S(shape, dtype):
    return jax.ShapeDtypeStruct(shape, dtype)


def vm_like(items):
    return [pltpu.VMEM(i.shape, i.dtype) for i in items]


def flat(ref, z=None):
    w = ref[...] if z is None else ref[z]
    return w.reshape(-1, w.shape[-1])


def cols(ref, lo, n):
    w = ref[:, :, :, :, lo : lo + n]
    return w.reshape(-1, n)


ZS, YS, XS = 4, 2, 2


def place():
    s = lax.axis_index("section")
    d = lax.axis_index("dp")
    return s, d // (YS * XS), (d // XS) % YS, d % XS


def at_chip(s, z, y, x):
    return (s, z * (YS * XS) + y * XS + x)


def partners(s, z, y, x):
    others = [at_chip(1 - s, z, y, x), at_chip(s, z, y, 1 - x), at_chip(s, z, 1 - y, x)]
    return others + [at_chip(s, (z + r) % ZS, y, x) for r in range(1, ZS)]


def greet(devices):
    barrier = pltpu.get_barrier_semaphore()
    for dev in devices:
        pl.semaphore_signal(barrier, inc=1, device_id=dev, device_id_type=MESH)
    pl.semaphore_wait(barrier, len(devices))


CHUNKS = ("vec", "wq", "wk", "wv", "wo", "u0", "u1", "dA", "dB")
NC = len(CHUNKS)
VL = 384


def mask_table(j):
    row = lax.broadcasted_iota(jnp.int32, (48, VL), 0)
    lane = lax.broadcasted_iota(jnp.int32, (48, VL), 1)
    one = [lane == 48 * (j % 8) + row] + [lane == 192 * (j % 2) + 4 * row + t for t in range(4)]
    return [m.astype(f32).astype(bf16) for m in one]


def front(lengths, inputs, masters, vec48):
    chunk = [(16, VL)] + [(48, D)] * 4 + [(48, FF // 2)] * 2 + [(192, 512), (192, 256)]
    saved = [S((LEN, D), bf16)] * 4 + [S((LEN, 128), f32), S((LEN, D), f32), S((LEN, FF), bf16), S((LEN, FF), bf16)]
    half = ZS // 2

    def kern(len_ref, x_h, mix, out, up, down, v48, *refs):
        full, refs = refs[:NC], refs[NC:]
        tabs, refs = refs[:2], refs[2:]
        (acto, pas), keep, refs = refs[:2], (refs[2:10], refs[10:18]), refs[18:]
        own, refs = refs[:NC], refs[NC:]
        wv, refs = refs[:NC], refs[NC:]
        x0, y0, y1, ab, q, k, v, ctx, lse, mid, act, dg, bup, send, recv, loc, lsem, ksem, asem, arecv = refs
        s, z, y, x = place()
        length = len_ref[s]
        near = partners(s, z, y, x)
        sib, px, py, pz = near[0], near[1], near[2], near[3:]
        x_in = pltpu.make_async_copy(x_h.at[s], x0, lsem.at[NC])
        x_in.start()
        greet(near)
        lo, hi = slice(0, half), slice(half, ZS)

        def copy(a, slot, idx, dev, source=None):
            dst = full[a].at[idx]
            return pltpu.make_async_remote_copy(
                src_ref=dst if source is None else source, dst_ref=dst, send_sem=send.at[a, slot],
                recv_sem=recv.at[a, slot], device_id=dev, device_id_type=MESH)

        def local(a):
            return pltpu.make_async_copy(own[a], full[a].at[s, z, y, x], loc.at[a])

        def prepare(a):
            if a == 0:
                maps = mask_table((z * YS + y) * XS + x)
                vb = v48[...].astype(bf16)
                own[0][...] = jnp.zeros_like(own[0])
                own[0][0:8, :] = tn(vb, maps[0])[0:8].astype(bf16)
                ups = sum(tn(vb, maps[1 + t])[8 + t : 9 + t] for t in range(4))
                own[0][8:16, :] = jnp.broadcast_to(ups, (8, VL)).astype(bf16)
            elif a < 4:
                own[a][...] = mix[:, (a - 1) * D : a * D].astype(bf16)
            elif a == 4:
                own[a][...] = out[...].astype(bf16)
            elif a < 7:
                own[a][...] = up[:, (a - 5) * (FF // 2) : (a - 4) * (FF // 2)].astype(bf16)
            else:
                own[a][...] = (down[:, 0:512] if a == 7 else down[:, 512:D]).astype(bf16)

        def first(a):
            local(a).start()
            for r in range(1, ZS):
                copy(a, r - 1, (s, z, y, x), pz[r - 1], own[a]).start()

        second_out = [(3, (s, lo, y, x), px), (4, (s, hi, y, x), py)]
        second_in = [(3, (s, lo, y, 1 - x), px), (4, (s, hi, 1 - y, x), py)]
        third_out = [(5, (s, lo, y), py), (6, (s, hi, slice(None), x), px)]
        third_in = [(5, (s, lo, 1 - y), py), (6, (s, hi, slice(None), 1 - x), px)]

        def waves(l):
            return [
                [(7, (l, slice(None), y, x), sib)],
                [(8, (l, lo, y, 1 - x), sib), (9, (l, hi, 1 - y, x), sib)],
                [(10, (l, lo, 1 - y), sib), (11, (l, hi, slice(None), 1 - x), sib)],
            ]

        def second(a):
            for r in range(1, ZS):
                copy(a, r - 1, (s, (z - r) % ZS, y, x), pz[r - 1]).wait_recv()
            local(a).wait()
            for c in second_out + waves(s)[0]:
                copy(a, *c).start()

        def third(a):
            for c in second_in:
                copy(a, *c).wait_recv()
            for c in third_out + waves(s)[1]:
                copy(a, *c).start()

        def last(a):
            for c in third_in:
                copy(a, *c).wait_recv()
            for c in waves(s)[2]:
                copy(a, *c).start()

        seen = set()

        def event(l, *what):
            todo = [w for w in what if (l, w) not in seen and w[1] < NC]
            seen.update((l, w) for w in todo)
            if todo:
                @pl.when(s == l)
                def _():
                    for stage, a in todo:
                        stage(a)

        def group(l, a):
            event(l, (third, a), (second, a + 2))

        def load(l, a):
            return pltpu.make_async_copy(full[a].at[l], wv[a], lsem.at[a])

        def complete(l, a):
            event(l, (last, a))

            @pl.when(s != l)
            def _():
                for wave in waves(l):
                    for c in wave:
                        copy(a, *c).wait_recv()
            load(l, a).start()
            load(l, a).wait()

        def store(l, i):
            if i == 0:
                return pltpu.make_async_copy(y0, pas, ksem.at[0])
            return pltpu.make_async_copy((q, k, v, ctx, lse, mid, act, dg)[i - 1], keep[l][i - 1], ksem.at[i])

        def show(l, local):
            src = (y0, y1)[l]
            if local:
                return pltpu.make_async_copy(src, acto.at[s], asem.at[l])
            return pltpu.make_async_remote_copy(
                src_ref=src, dst_ref=acto.at[s], send_sem=asem.at[l], recv_sem=arecv.at[0], device_id=sib, device_id_type=MESH)

        kb = jnp.where(lax.broadcasted_iota(jnp.int32, (1, LEN), 1) < length, 0.0, -1e30).astype(f32)
        tri = lax.broadcasted_iota(jnp.int32, (RB, RB), 1) <= lax.broadcasted_iota(jnp.int32, (RB, RB), 0)
        lane = lax.broadcasted_iota(jnp.int32, (RB, 128), 1)

        def layer(l, xin, yout):
            vec = tabs[l]

            def settle(i):
                if l:
                    store(0, i).wait()

            complete(l, 0)
            pv = wv[0][...].reshape(16, 16, VL).astype(f32)
            vec[:, 0:VL] = sum(pv[j, 0:8] for j in range(8))
            vec[:, VL:D] = sum(pv[j, 0:8] for j in range(8, 16))
            for m in range(8):
                bup[:, m * VL : (m + 1) * VL] = pv[2 * m, 8:16] + pv[2 * m + 1, 8:16]

            def norm1(i, _):
                r = rows_of(i)
                xh, _r = norm_parts(xin[r, :].astype(f32))
                ab[r, :] = (xh * vec[0:1, :] + vec[1:2, :]).astype(bf16)
                return 0

            lax.fori_loop(0, NB, norm1, 0)

            def project(a, dst, f):
                def step(i, _):
                    r = rows_of(i)
                    dst[r, :] = f(nn(ab[r, :], flat(wv[a]))).astype(bf16)
                    return 0

                lax.fori_loop(0, NB, step, 0)

            complete(l, 1)
            group(l, 3)
            settle(1)
            project(1, q, lambda t: (t + vec[2:3, :]).astype(bf16).astype(f32) * 0.125)
            store(l, 1).start()
            complete(l, 2)
            group(l, 4)
            settle(2)
            project(2, k, lambda t: t)
            store(l, 2).start()
            complete(l, 3)
            group(l, 5)
            settle(3)
            project(3, v, lambda t: t + vec[3:4, :])
            store(l, 3).start()
            settle(4)
            settle(5)
            lse[...] = jnp.zeros_like(lse)

            def att(p, _):
                @pl.when(p == 1)
                def _():
                    group(l, 6)

                @pl.when(p == 2)
                def _():
                    event(l, (last, 4))

                @pl.when(p == 5)
                def _():
                    group(l, 7)
                    event(l, (last, 5))

                c = pl.ds(pl.multiple_of(p * 128, 128), 128)
                for i in range(NB):
                    top = i * RB
                    r = slice(top, top + RB)
                    qp = q[r, c]
                    outs = []
                    ls = []
                    for h in range(2):
                        qh = jnp.where((lane < 64) == (h == 0), qp, jnp.zeros_like(qp))
                        sd = jnp.where(tri, nt(qh, k[r, c]) + kb[:, top : top + RB], -1e30)
                        m = jnp.max(sd, -1, keepdims=True)
                        if i:
                            sl = nt(qh, k[0:top, c]) + kb[:, 0:top]
                            m = jnp.maximum(m, jnp.max(sl, -1, keepdims=True))
                        ed = jnp.exp(sd - m)
                        tot = jnp.sum(ed, -1, keepdims=True)
                        o = nn(ed.astype(bf16), v[r, c])
                        if i:
                            el = jnp.exp(sl - m)
                            tot = tot + jnp.sum(el, -1, keepdims=True)
                            o = o + nn(el.astype(bf16), v[0:top, c])
                        outs.append(o * (1.0 / tot))
                        ls.append(m + jnp.log(tot))
                    ctx[r, c] = jnp.where(lane < 64, outs[0], outs[1]).astype(bf16)
                    lse[r, :] = jnp.where(lane == 2 * p, ls[0], jnp.where(lane == 2 * p + 1, ls[1], lse[r, :]))
                return 0

            lax.fori_loop(0, D // 128, att, 0)
            store(l, 4).start()
            store(l, 5).start()
            if l == 0:
                event(1, *[(first, a) for a in range(NC)])
            complete(l, 4)
            settle(6)

            def middle(i, _):
                r = rows_of(i)
                md = xin[r, :].astype(f32) + nn(ctx[r, :], flat(wv[4])) + vec[4:5, :]
                mid[r, :] = md
                xh, _r = norm_parts(md)
                ab[r, :] = (xh * vec[5:6, :] + vec[6:7, :]).astype(bf16)
                return 0

            lax.fori_loop(0, NB, middle, 0)
            store(l, 6).start()
            settle(7)
            settle(8)
            for a in (5, 6):
                complete(l, a)
                if a == 5:
                    group(l, 8)

                def expand(i, _):
                    r = rows_of(i)
                    for j in range(2):
                        off = (a - 5) * (FF // 2) + j * FB
                        cc = slice(off, off + FB)
                        h = nn(ab[r, :], cols(wv[a], j * FB, FB)) + bup[0:1, cc]
                        h2 = h * h
                        t = jnp.tanh(h * (K0 + (K0 * K1) * h2))
                        hf = 0.5 + 0.5 * t
                        act[r, cc] = (h * hf).astype(bf16)
                        dg[r, cc] = (hf + (0.5 * h) * (1.0 - t * t) * (K0 + (3 * K0 * K1) * h2)).astype(bf16)
                    return 0

                lax.fori_loop(0, NB, expand, 0)
            store(l, 7).start()
            store(l, 8).start()
            if l == 0:
                event(1, (second, 0), (second, 1), (second, 2))
            for a, lo_, hi_ in ((7, 0, 512), (8, 512, D)):
                complete(l, a)
                if l == 0:
                    event(1, *([(third, 0), (third, 1), (second, 3)] if a == 7 else [(third, 2), (second, 4)]))

                def contract(i, _):
                    r = rows_of(i)
                    t = mid[r, lo_:hi_] + nn(act[r, :], flat(wv[a])) + vec[7:8, lo_:hi_]
                    yout[r, lo_:hi_] = t.astype(bf16)
                    return 0

                lax.fori_loop(0, NB, contract, 0)
            if l == 0:
                store(l, 0).start()

            @pl.when(s == l)
            def _():
                show(l, True).start()

            @pl.when(s != l)
            def _():
                show(l, False).start()

        for a in range(NC):
            prepare(a)
            event(0, (first, a))
        event(0, (second, 0), (second, 1), (second, 2), (third, 0), (third, 1), (second, 3), (third, 2), (second, 4))
        x_in.wait()
        layer(0, x0, y0)
        layer(1, y0, y1)
        store(0, 0).wait()
        for i in range(1, 9):
            store(1, i).wait()
        for l in range(2):
            @pl.when(s == l)
            def _():
                show(l, True).wait()
                show(l, False).wait_recv()

            @pl.when(s != l)
            def _():
                show(l, False).wait_send()
        for a in range(NC):
            for r in range(1, ZS):
                copy(a, r - 1, (s, z, y, x), pz[r - 1], own[a]).wait_send()
            for c in second_out + third_out + sum(waves(s), []):
                copy(a, *c).wait_send()

    outs = [S((2, ZS, YS, XS) + c, bf16) for c in chunk] + [S((8, D), f32)] * 2 + [S((2, LEN, D), bf16), S((LEN, D), bf16)] + saved * 2
    act_ = [S((LEN, D), bf16)] * 4 + saved + [S((8, FF), f32)]
    return pl.pallas_call(
        kern,
        out_shape=outs,
        in_specs=[SM, AN] + [VM] * 5,
        out_specs=[AN] * NC + [VM] * 2 + [AN] * 18,
        scratch_shapes=vm_like([S(c, bf16) for c in chunk] + [S((ZS, YS, XS) + c, bf16) for c in chunk] + act_)
        + [pltpu.SemaphoreType.DMA((NC, 12)), pltpu.SemaphoreType.DMA((NC, 12)), pltpu.SemaphoreType.DMA((NC,)), pltpu.SemaphoreType.DMA((NC + 1,)), pltpu.SemaphoreType.DMA((9,)), pltpu.SemaphoreType.DMA((2,)), pltpu.SemaphoreType.DMA((1,))],
        compiler_params=pltpu.CompilerParams(collective_id=1, has_side_effects=True, vmem_limit_bytes=60 * MIB),
        name="front",
    )(lengths, inputs, *masters, vec48)


TILES = (4, 2, 2, 1, 1, 1, 1, 1)
NG = len(TILES)


def back(lengths, inputs, cotangent, passed, weights, tables, saved):
    half = ZS // 2
    HW = D // 2
    blk = [(192, HW), (48, D), (48, D)] + [(48, HW)] * 4 + [(8, HW)]
    typ = [bf16] * 7 + [f32]
    sn = ("q", "k", "v", "ctx", "lse", "mid", "act", "dg")

    def kern(len_ref, tab0, tab1, x_h, cot_h, pas_h, *refs):
        wh, refs = dict(zip(CHUNKS[1:], refs[:8])), refs[8:]
        sh, refs = (dict(zip(sn, refs[:8])), dict(zip(sn, refs[8:16]))), refs[16:]
        dxo, fmix, fout, fup, fdown, fvec, total = refs[:7]
        refs = refs[7:]
        u0, u1, dA, dB, wo, dh, gm, mids, g, ga, dctx, t3, lse, dkT, dvT, lT, gvec, gbup = refs[:18]
        refs = refs[18:]
        own, sibs, a2, b2, a3, b3, r4, fs, fr = [refs[k * NG : (k + 1) * NG] for k in range(9)]
        stD, stU, stV, fo, norms, sq, lsem, dsem, drecv, ssem, srecv, send, recv, fsend, frecv, nsend, nrecv, credit = refs[9 * NG :]
        s, z, y, x = place()
        length = len_ref[s]
        near = partners(s, z, y, x)
        sib, px, py, pz = near[0], near[1], near[2], near[3:]
        lo, hi = slice(0, half), slice(half, ZS)
        wv = dict(u0=u0, u1=u1, dA=dA, dB=dB, wo=wo)
        names = ("dg", "dA", "dB", "u0", "u1", "wo", "lse", "q", "k", "v", "ctx", "x", "wq", "wk", "wv", "a0", "a1", "a2", "a3", "g")
        slot = {n: k for k, n in enumerate(names)}

        def load(l, n):
            if n in wv:
                a, b = wh[n].at[l], wv[n]
            elif n in ("wq", "wk", "wv"):
                a, b = wh[n].at[l], {"wq": u0.at[:, :, :, :, 0:D], "wk": u0.at[:, :, :, :, D : 2 * D], "wv": u1.at[:, :, :, :, 0:D]}[n]
            elif n == "x":
                a, b = (x_h.at[s], pas_h)[l], ga
            elif n == "g":
                a, b = cot_h.at[s], g
            elif n[0] == "a":
                k = int(n[1])
                a, b = sh[l]["act"].at[:, k * D : (k + 1) * D], t3.at[k % 3]
            else:
                a, b = sh[l][n], dict(dg=dh, lse=lse, q=t3.at[0], k=t3.at[1], v=t3.at[2], ctx=t3.at[1])[n]
            return pltpu.make_async_copy(a, b, lsem.at[slot[n]])

        def start(l, *ns):
            for n in ns:
                load(l, n).start()

        def ready(l, *ns):
            for n in ns:
                load(l, n).wait()

        def mid_load(l, i):
            r = pl.ds(pl.multiple_of(i * RB, RB), RB)
            return pltpu.make_async_copy(sh[l]["mid"].at[r, :], mids.at[lax.rem(i, 2)], lsem.at[len(names) + lax.rem(i, 2)])

        start(1, "g", "dg", "dA", "dB", "u0", "u1", "wo", "lse", "a0", "a1", "a2")
        greet(near)

        def copy(a, k, src, dst, dev):
            return pltpu.make_async_remote_copy(
                src_ref=src, dst_ref=dst, send_sem=send.at[a, k], recv_sem=recv.at[a, k], device_id=dev, device_id_type=MESH)

        def give(a, k, dev):
            pl.semaphore_signal(credit.at[a, k], inc=1, device_id=dev, device_id_type=MESH)

        def take(a, *ks):
            for k in ks:
                pl.semaphore_wait(credit.at[a, k], 1)

        def second(a):
            return [copy(a, 0, own[a].at[lo, 1 - y], a2[a], py), copy(a, 1, own[a].at[hi, :, 1 - x], b2[a], px)]

        def third(a):
            return [copy(a, 2, own[a].at[lo, y, 1 - x], a3[a], px), copy(a, 3, own[a].at[hi, 1 - y, x], b3[a], py)]

        def fourth(a):
            return [copy(a, 3 + r, own[a].at[(z + r) % ZS, y, x], r4[a].at[r - 1], pz[r - 1]) for r in range(1, ZS)]

        first_tile = [sum(TILES[:a]) for a in range(NG)]

        def to_sib(a, t, src=None):
            if a == 0:
                src, dst = stD.at[t % 2] if src is None else src, sibs[0].at[t]
            elif a < 3:
                src, dst = stU.at[t % 2] if src is None else src, sibs[a].at[:, :, :, :, t * HW : (t + 1) * HW]
            elif a < 7:
                src, dst = stU.at[a % 2], sibs[a]
            else:
                src, dst = stV, sibs[a]
            n = first_tile[a] + t
            return pltpu.make_async_remote_copy(
                src_ref=src, dst_ref=dst, send_sem=ssem.at[n], recv_sem=srecv.at[n], device_id=sib, device_id_type=MESH)

        def add(ref, idx, other, oidx):
            ref[idx] = (ref[idx].astype(f32) + other[oidx].astype(f32)).astype(ref.dtype)

        def one(l, a):
            for t in range(TILES[a]):
                to_sib(a, t).wait_recv()

            def step(i, _):
                idx = (i // (YS * XS), (i // XS) % YS, i % XS)
                add(own[a], idx, sibs[a], idx)
                return 0

            lax.fori_loop(0, ZS * YS * XS, step, 0)
            if l:
                give(a, 0, sib)
            else:
                take(a, 1, 2)
            for c in second(a):
                c.start()

        def two(l, a):
            for c in second(a):
                c.wait()

            def step(i, _):
                h, k = i // 2, i % 2
                add(own[a], (h, y, k), a2[a], (h, k))
                add(own[a], (half + h, k, x), b2[a], (h, k))
                return 0

            lax.fori_loop(0, half * 2, step, 0)
            if l:
                give(a, 1, py)
                give(a, 2, px)
            else:
                take(a, 3, 4)
            for c in third(a):
                c.start()

        def three(l, a):
            for c in third(a):
                c.wait()

            def step(h, _):
                add(own[a], (h, y, x), a3[a], (h,))
                add(own[a], (half + h, y, x), b3[a], (h,))
                return 0

            lax.fori_loop(0, half, step, 0)
            if l:
                give(a, 3, px)
                give(a, 4, py)
            else:
                take(a, 5, 6, 7)
            for c in fourth(a):
                c.start()

        def put(a, v, h):
            def at(base, n):
                return pl.ds(pl.multiple_of(base + h * n, n), n)

            if a == 0:
                fdown[:, at(0, HW)] = v
            elif a < 3:
                for t in range(2):
                    fup[:, at(((a - 1) * 2 + t) * D, HW)] = v[:, t * HW : (t + 1) * HW]
            elif a == 3:
                fout[:, at(0, HW)] = v
            elif a < 7:
                for t in range(3):
                    fmix[:, at(t * D + (a - 4) * 256, 128)] = v[:, t * 128 : (t + 1) * 128]

        def finish(a):
            return pltpu.make_async_remote_copy(
                src_ref=fs[a], dst_ref=fr[a], send_sem=fsend.at[a], recv_sem=frecv.at[a], device_id=sib, device_id_type=MESH)

        def four(l, a):
            for c in fourth(a):
                c.wait()
            v = own[a][z, y, x].astype(f32)
            for r in range(ZS - 1):
                v = v + r4[a][r].astype(f32)
            if l:
                for r in range(1, ZS):
                    give(a, 4 + r, at_chip(s, (z - r) % ZS, y, x))
            if a < 7:
                sq[...] = sq[...] + jnp.sum(v * v)

            @pl.when(s == l)
            def _():
                if a < 7:
                    put(a, v, s)
                else:
                    fo[...] = v

            @pl.when(s != l)
            def _():
                fs[a][...] = v
                finish(a).start()

        def event(*todo):
            for l, stage, a in todo:
                stage(l, a)

        kb = jnp.where(lax.broadcasted_iota(jnp.int32, (1, LEN), 1) < length, 0.0, -1e30).astype(f32)
        tri = lax.broadcasted_iota(jnp.int32, (RB, RB), 1) <= lax.broadcasted_iota(jnp.int32, (RB, RB), 0)
        lane = lax.broadcasted_iota(jnp.int32, (RB, 128), 1)

        def cs(t):
            return jnp.sum(t, 0, keepdims=True)

        def parts(v, cut):
            vb = v.astype(bf16)
            a = jnp.concatenate([vb[:, c : c + w] for c, w in cut[0]], 1) if len(cut[0]) > 1 else vb[:, 0:HW]
            b = jnp.concatenate([vb[:, c : c + w] for c, w in cut[1]], 1) if len(cut[1]) > 1 else vb[:, HW:D]
            return jnp.where(s == 0, a, b), jnp.where(s == 0, b, a)

        straight = ([(0, HW)], [(HW, HW)])
        woven = tuple([(256 * t + 128 * h, 128) for t in range(3)] for h in range(2))

        def dx_copy(l, i, local):
            r = slice(i * RB, (i + 1) * RB)
            if local:
                return pltpu.make_async_copy(gm.at[r, :], dxo.at[s, r, :], dsem.at[i])
            return pltpu.make_async_remote_copy(
                src_ref=gm.at[r, :], dst_ref=dxo.at[s, r, :], send_sem=dsem.at[i], recv_sem=drecv.at[i], device_id=sib, device_id_type=MESH)

        def dx_wait(l, i):
            @pl.when(s == l)
            def _():
                dx_copy(l, i, True).wait()

            @pl.when(s != l)
            def _():
                dx_copy(l, i, False).wait_send()

        def at(l, where):
            if where in plan:
                event(*[(l, st, a) for st, a in plan[where]])
            if l == 0 and where in rest:
                event(*[(1, st, a) for st, a in rest[where]])

        plan = {
            "u1": [(one, 0)], "u3": [(one, 1)], "o": [(one, 2)], "p0": [(one, 3)], "p2": [(one, 4), (two, 0)], "p3": [(two, 1)],
            "p4": [(one, 5)], "p5": [(two, 2)], "m": [(two, 3), (one, 6)], "r1": [(three, 0)], "r2": [(three, 1)], "r3": [(two, 4)],
        }
        rest = {
            "s0": [(one, 7), (two, 5), (three, 2)], "s1": [(two, 6), (three, 3)], "s2": [(four, 0), (two, 7), (three, 4)], "s3": [(four, 1), (three, 5)],
            "d0": [(three, 6)], "d1": [(three, 7)], "d2": [(four, 2)], "d3": [(four, 3)], "p1": [(four, 4), (four, 5), (four, 6), (four, 7)],
        }
        ending = [(one, 7), (two, 5), (three, 2), (four, 0), (two, 6), (three, 3), (four, 1), (two, 7), (three, 4), (four, 2), (three, 5), (four, 3),
                  (three, 6), (three, 7), (four, 4), (four, 5), (four, 6), (four, 7)]

        last_send = {}

        def send_tile(l, a, t, key, write):
            if key in last_send:
                to_sib(*last_send[key]).wait_send()
            write()
            if l == 0 and t == 0:
                take(a, 0)
            to_sib(a, t).start()
            last_send[key] = (a, t)

        def layer(l):
            vec = (tab0, tab1)[l]
            gvec[...] = jnp.zeros_like(gvec)
            gbup[...] = jnp.zeros_like(gbup)
            mid_load(l, 0).start()
            ready(l, "dg", "dA", "dB", "wo", "u0", "u1")
            if l:
                ready(l, "g")

            def st1(i, _):
                r = rows_of(i)

                @pl.when(i + 1 < NB)
                def _():
                    mid_load(l, i + 1).start()

                gb = g[r, :]
                if l:
                    pos = i * RB + lax.broadcasted_iota(jnp.int32, (RB, D), 0)
                    gb = jnp.where(pos < length, gb.astype(f32), 0.0).astype(bf16)
                    g[r, :] = gb
                gf = gb.astype(f32)
                dc = jnp.zeros((RB, D), f32)
                for j in range(FF // FB):
                    cc = slice(j * FB, (j + 1) * FB)
                    d = ((nt(gb[:, 0:512], flat(dA, j)) + nt(gb[:, 512:], flat(dB, j))) * dh[r, cc].astype(f32)).astype(bf16)
                    dh[r, cc] = d
                    gbup[0:1, cc] += cs(d.astype(f32))
                    dc = dc + nt(d, cols((u0, u1)[j // 2], (j % 2) * FB, FB))
                if l == 0:
                    for k in range(NB):
                        @pl.when(i == k)
                        def _(k=k):
                            at(0, "s%d" % k)
                            dx_wait(1, k)
                mid_load(l, i).wait()
                xh, rstd = norm_parts(mids[lax.rem(i, 2)])
                lT[:, r] = (xh * vec[5:6, :] + vec[6:7, :]).T.astype(bf16)
                e = dc * vec[5:6, :]
                gmv = gf + (e - jnp.mean(e, -1, keepdims=True) - xh * jnp.mean(e * xh, -1, keepdims=True)) * rstd
                gm[r, :] = gmv
                gav = gmv.astype(bf16)
                ga[r, :] = gav
                gvec[4:5, :] += cs(gav.astype(f32))
                gvec[5:6, :] += cs(dc * xh)
                gvec[6:7, :] += cs(dc)
                gvec[7:8, :] += cs(gf)
                dctx[r, :] = nt(gav, flat(wo)).astype(bf16)
                return 0

            lax.fori_loop(0, NB, st1, 0)
            if l:
                start(0, "dA", "dB", "wo")
            start(l, "wq", "wk", "wv")
            for t in range(ZS):
                ready(l, "a%d" % t)

                def write(t=t):
                    for m in range(2):
                        mine, other = parts(tn(t3[t % 3, :, m * HW : (m + 1) * HW], g[...]), straight)
                        own[0][t, m] = mine.reshape(2, 192, HW)
                        stD[t % 2, m] = other.reshape(2, 192, HW)

                send_tile(l, 0, t, ("D", t % 2), write)
                if t == 0:
                    start(l, "a3")
                if t == 1:
                    start(l, "ctx")
                at(l, "d%d" % t)
            start(l, "v")
            for t in range(4):
                a = 1 + t // 2

                def write(t=t, a=a):
                    for m in range(2):
                        v = nn(lT[m * HW : (m + 1) * HW, :], dh[:, t * D : (t + 1) * D])
                        mine, other = parts(v, straight)
                        w = slice((t % 2) * HW, (t % 2 + 1) * HW)
                        own[a][2 * m : 2 * m + 2, :, :, :, w] = mine.reshape(2, 2, 2, 48, HW)
                        stU[t % 2, 2 * m : 2 * m + 2] = other.reshape(2, 2, 2, 48, HW)

                send_tile(l, a, t % 2, ("U", t % 2), write)
                at(l, "u%d" % t)
            start(l, "q")
            if l:
                start(0, "dg")
            ready(l, "ctx")

            def write_out():
                for m in range(2):
                    mine, other = parts(tn(t3[1, :, m * HW : (m + 1) * HW], ga[...]), straight)
                    own[3][2 * m : 2 * m + 2] = mine.reshape(2, 2, 2, 48, HW)
                    stU[1, 2 * m : 2 * m + 2] = other.reshape(2, 2, 2, 48, HW)

            send_tile(l, 3, 0, ("U", 1), write_out)
            start(l, "k", "x")
            at(l, "o")
            ready(l, "x")

            def norm1(i, _):
                r = rows_of(i)
                xh, _r = norm_parts(ga[r, :].astype(f32))
                lT[:, r] = (xh * vec[0:1, :] + vec[1:2, :]).T.astype(bf16)
                return 0

            lax.fori_loop(0, NB, norm1, 0)
            ready(l, "q", "k", "v", "lse")

            def pair(p):
                c = pl.ds(pl.multiple_of(p * 128, 128), 128)
                dkT[...] = jnp.zeros_like(dkT)
                dvT[...] = jnp.zeros_like(dvT)
                for i in range(NB):
                    top = i * RB
                    r = slice(top, top + RB)
                    qp = t3[0, r, c]
                    dcp = dctx[r, c]
                    lr = lse[r, :]
                    qT = qp.astype(f32).T.astype(bf16)
                    dcT = dcp.astype(f32).T.astype(bf16)
                    dq = None
                    for h in range(2):
                        sel = (lane < 64) == (h == 0)
                        qh = jnp.where(sel, qp, jnp.zeros_like(qp))
                        dch = jnp.where(sel, dcp, jnp.zeros_like(dcp))
                        ls = jnp.sum(jnp.where(lane == 2 * p + h, lr, 0.0), -1, keepdims=True)
                        hs = slice(h * 64, h * 64 + 64)
                        pd = jnp.exp(jnp.where(tri, nt(qh, t3[1, r, c]) + kb[:, top : top + RB], -1e30) - ls)
                        dpd = nt(dch, t3[2, r, c])
                        delta = jnp.sum(pd * dpd, -1, keepdims=True)
                        if i:
                            plft = jnp.exp(nt(qh, t3[1, 0:top, c]) + kb[:, 0:top] - ls)
                            dpl = nt(dch, t3[2, 0:top, c])
                            delta = delta + jnp.sum(plft * dpl, -1, keepdims=True)
                        dsd = (pd * (dpd - delta)).astype(bf16)
                        dkT[hs, r] += nn(qT[hs], dsd)
                        dvT[hs, r] += nn(dcT[hs], pd.astype(bf16))
                        t = nn(dsd, t3[1, r, c])
                        if i:
                            dsl = (plft * (dpl - delta)).astype(bf16)
                            dkT[hs, 0:top] += nn(qT[hs], dsl)
                            dvT[hs, 0:top] += nn(dcT[hs], plft.astype(bf16))
                            t = t + nn(dsl, t3[1, 0:top, c])
                        dq = t if h == 0 else jnp.where(lane < 64, dq, t)
                    t3[0, r, c] = (dq * 0.125).astype(bf16)
                t3[1, :, c] = dkT[...].T.astype(bf16)
                t3[2, :, c] = dvT[...].T.astype(bf16)

            def two_pairs(kk, _):
                for b in range(2):
                    for k in range(3):
                        @pl.when(kk == k)
                        def _(k=k):
                            at(l, "p%d" % (2 * k + b))
                    pair(2 * kk + b)
                c2 = pl.ds(pl.multiple_of(kk * 256, 256), 256)
                for k in range(3):
                    @pl.when(kk == k)
                    def _(k=k):
                        def write():
                            for m in range(2):
                                v = jnp.concatenate([nn(lT[m * HW : (m + 1) * HW, :], t3[t, :, k * 256 : (k + 1) * 256]) for t in range(3)], 1)
                                mine, other = parts(v, woven)
                                own[4 + k][2 * m : 2 * m + 2] = mine.reshape(2, 2, 2, 48, HW)
                                stU[k % 2, 2 * m : 2 * m + 2] = other.reshape(2, 2, 2, 48, HW)

                        send_tile(l, 4 + k, 0, ("U", k % 2), write)
                return 0

            lax.fori_loop(0, 3, two_pairs, 0)
            at(l, "m")
            ready(l, "wq", "wk", "wv")

            def st3(i, _):
                r = rows_of(i)
                for k in range(NB):
                    @pl.when(i == k)
                    def _(k=k):
                        at(l, "r%d" % k)
                dq, dk, dv = t3[0, r, :], t3[1, r, :], t3[2, r, :]
                gvec[2:3, :] += cs(dq.astype(f32))
                gvec[3:4, :] += cs(dv.astype(f32))
                da = nt(dq, cols(u0, 0, D)) + nt(dk, cols(u0, D, D)) + nt(dv, cols(u1, 0, D))
                xh, rstd = norm_parts(ga[r, :].astype(f32))
                gvec[0:1, :] += cs(da * xh)
                gvec[1:2, :] += cs(da)
                e = da * vec[0:1, :]
                o = gm[r, :] + (e - jnp.mean(e, -1, keepdims=True) - xh * jnp.mean(e * xh, -1, keepdims=True)) * rstd
                gm[r, :] = o
                g[r, :] = o.astype(bf16)
                for k in range(NB):
                    @pl.when((i == k) & (s == l))
                    def _(k=k):
                        dx_copy(l, k, True).start()

                    @pl.when((i == k) & (s != l))
                    def _(k=k):
                        dx_copy(l, k, False).start()
                return 0

            lax.fori_loop(0, NB, st3, 0)
            if l:
                start(0, "u0", "u1", "lse", "a0", "a1", "a2")

            def write_vec():
                for j in range(ZS * YS * XS):
                    idx = (j // 4, (j // 2) % 2, j % 2)
                    tab = gvec[:, (j // 8) * HW : (j // 8 + 1) * HW]
                    ups = jnp.broadcast_to(gbup[0:1, (j // 2) * HW : (j // 2 + 1) * HW], (8, HW))
                    own[7][idx] = jnp.where(s == 0, tab, ups)
                    stV[idx] = jnp.where(s == 0, ups, tab)

            send_tile(l, 7, 0, "V", write_vec)

        sq[...] = jnp.zeros_like(sq)
        layer(1)
        layer(0)
        event(*[(0, st, a) for st, a in ending])
        for a in range(NG):
            finish(a).wait()
            if a < 7:
                put(a, fr[a][...], 1 - s)
        tab = jnp.where(s == 0, fo[...], fr[7][...])
        ups = jnp.where(s == 0, fr[7][...], fo[...])
        j = (z * YS + y) * XS + x
        row = lax.broadcasted_iota(jnp.int32, (48, HW), 0)
        ln = lax.broadcasted_iota(jnp.int32, (48, HW), 1)
        col = lax.broadcasted_iota(jnp.int32, (48, TABLE), 1)
        vals = jnp.zeros((48, TABLE), f32)
        for k in range(TABLE):
            if k < 8:
                got = jnp.sum(jnp.where(ln == 48 * (j % 8) + row, tab[k : k + 1], 0.0), -1, keepdims=True)
            else:
                got = jnp.sum(jnp.where(ln == 192 * (j % 2) + 4 * row + (k - 8), ups[0:1], 0.0), -1, keepdims=True)
            vals = jnp.where(col == k, got, vals)
        fvec[...] = vals
        norms[0] = sq[...] + jnp.sum(vals * vals)

        def shared(k, dev, into):
            return pltpu.make_async_remote_copy(
                src_ref=norms.at[k], dst_ref=norms.at[into], send_sem=nsend.at[into], recv_sem=nrecv.at[into], device_id=dev, device_id_type=MESH)

        for k, dev in enumerate((sib, px, py)):
            c = shared(2 * k, dev, 2 * k + 1)
            c.start()
            c.wait()
            norms[2 * k + 2] = norms[2 * k] + norms[2 * k + 1]
        cs_ = [shared(6, pz[r], 7 + r) for r in range(ZS - 1)]
        for c in cs_:
            c.start()
        for c in cs_:
            c.wait()
        total[...] = norms[6] + norms[7] + norms[8] + norms[9]
        for i in range(NB):
            dx_wait(0, i)
            dx_copy(0, i, False).wait_recv()
        for key, (a, t) in last_send.items():
            to_sib(a, t).wait_send()

    def bufs(lead):
        return [S(lead + blk[a], typ[a]) for a in range(NG)]

    w5 = [S(w.shape[1:], bf16) for w in weights]
    work = [w5[4], w5[5], w5[6], w5[7], w5[3], S((LEN, FF), bf16), S((LEN, D), f32), S((2, RB, D), f32)] + [S((LEN, D), bf16)] * 3
    work += [S((3, LEN, D), bf16), S((LEN, 128), f32), S((128, LEN), f32), S((128, LEN), f32), S((D, LEN), bf16), S((8, D), f32), S((8, FF), f32)]
    for lead in ((ZS, YS, XS), (ZS, YS, XS), (half, XS), (half, YS), (half,), (half,), (ZS - 1,)):
        work += bufs(lead)
    work += [S(b, f32) for b in blk] * 2
    work += [S((2, 2, 2, 192, HW), bf16), S((2, ZS, YS, XS, 48, HW), bf16), S((ZS, YS, XS, 8, HW), f32), S((8, HW), f32), S((10, 8, 128), f32), S((8, 128), f32)]
    dma = pltpu.SemaphoreType.DMA
    nt_ = sum(TILES)
    sems = [dma((22,)), dma((NB,)), dma((NB,)), dma((nt_,)), dma((nt_,)), dma((NG, 7)), dma((NG, 7)), dma((NG,)), dma((NG,)), dma((10,)), dma((10,)), pltpu.SemaphoreType.REGULAR((NG, 8))]
    outs = [S((2, LEN, D), f32), S((48, 3 * D), f32), S((48, D), f32), S((48, FF), f32), S((192, D), f32), S((48, TABLE), f32), S((8, 128), f32)]
    return pl.pallas_call(
        kern,
        out_shape=outs,
        in_specs=[SM, VM, VM] + [AN] * 27,
        out_specs=[AN] + [VM] * 6,
        scratch_shapes=vm_like(work) + sems,
        compiler_params=pltpu.CompilerParams(collective_id=2, has_side_effects=True, vmem_limit_bytes=64 * MIB - 65536),
        name="back",
    )(lengths, *tables, inputs, cotangent, passed, *weights, *saved[0], *saved[1])


RATES = (0.05, 0.25, 0.05, 0.05, 0.5)
DECAYS = (0.1, 0.1, 0.1, 0.1, 0.0)


def adam(total, grads, masters, firsts, seconds, whole):
    n = len(grads)
    flat_ = [a for four in zip(grads, masters, firsts, seconds) for a in four]
    steps = 6
    nw = len(whole)

    def spec(a):
        if a.shape[0] % (8 * steps):
            return pl.BlockSpec(a.shape, lambda i: (0, 0))
        return pl.BlockSpec((a.shape[0] // steps, a.shape[1]), lambda i: (i, 0))

    def kern(t, *refs):
        src, refs = refs[:nw], refs[nw:]
        ins, refs = refs[: 4 * n], refs[4 * n :]
        outs, dst, refs = refs[: 3 * n], refs[3 * n : 3 * n + nw], refs[3 * n + nw :]
        hold, sem = refs[:nw], refs[nw]
        into = [pltpu.make_async_copy(src[i], hold[i], sem.at[i]) for i in range(nw)]
        cps = [pltpu.make_async_copy(hold[i], dst[i].at[0], sem.at[i]) for i in range(nw)]

        @pl.when(pl.program_id(0) == 0)
        def _():
            for c in into:
                c.start()

        @pl.when(pl.program_id(0) == 2)
        def _():
            for i in range(nw):
                into[i].wait()
                cps[i].start()

        norm = jnp.sqrt(t[0:1, 0:1])
        factor = jnp.minimum(1.0, 1.0 / (norm + 1e-06))
        for i in range(n):
            gr, w, m, u = (r[...] for r in ins[4 * i : 4 * i + 4])
            mo, uo, wo = outs[3 * i : 3 * i + 3]
            gr = gr * factor
            m1 = 0.9 * m + (1.0 - 0.9) * gr
            u1 = 0.999 * u + (1.0 - 0.999) * gr * gr
            mh = m1 / (1.0 - 0.9**STEP)
            uh = u1 / (1.0 - 0.999**STEP)
            mo[...] = m1
            uo[...] = u1
            wo[...] = w - RATES[i] * (mh / (jnp.sqrt(uh) + 1e-08) + DECAYS[i] * w)

        @pl.when(pl.program_id(0) == steps - 1)
        def _():
            for c in cps:
                c.wait()

    outs = [S(a.shape, f32) for a in masters for _ in range(3)]
    return pl.pallas_call(
        kern,
        grid=(steps,),
        out_shape=outs + [S((1,) + w.shape, w.dtype) for w in whole],
        in_specs=[pl.BlockSpec((8, 128), lambda i: (0, 0))] + [AN] * nw + [spec(a) for a in flat_],
        out_specs=[spec(a) for a in outs] + [AN] * nw,
        scratch_shapes=vm_like(whole) + [pltpu.SemaphoreType.DMA((nw,))],
        compiler_params=pltpu.CompilerParams(vmem_limit_bytes=62 * MIB),
        name="adam",
    )(total, *whole, *flat_)


def swap(v):
    return lax.ppermute(v, "section", [(0, 1), (1, 0)])


def plain_fwd(x, length, weights, vec, bup):
    mix, out, up, down = weights
    row = lambda i: vec[i][None]
    xf = x.astype(f32)
    a = (norm_parts(xf)[0] * row(0) + row(1)).astype(bf16)
    m = nn(a, mix)
    q = ((m[:, :D] + row(2)).astype(bf16).astype(f32) * 0.125).astype(bf16)
    k = m[:, D : 2 * D].astype(bf16)
    v = (m[:, 2 * D :] + row(3)).astype(bf16)
    heads = [t.reshape(LEN, D // 64, 64) for t in (q, k, v)]
    sc = jnp.einsum("qhe,khe->hqk", heads[0], heads[1], preferred_element_type=f32)
    pos = jnp.arange(LEN)
    sc = jnp.where(((pos[None, :] <= pos[:, None]) & (pos[None, :] < length[0]))[None], sc, -1e30)
    top = jnp.max(sc, -1, keepdims=True)
    e = jnp.exp(sc - top)
    tot = jnp.sum(e, -1, keepdims=True)
    ctx = jnp.einsum("hqk,khe->qhe", (e / tot).astype(bf16), heads[2], preferred_element_type=f32).reshape(LEN, D).astype(bf16)
    lse = jnp.pad((top + jnp.log(tot))[:, :, 0].T, ((0, 0), (0, 128 - D // 64)))
    mid = xf + nn(ctx, out) + row(4)
    c = (norm_parts(mid)[0] * row(5) + row(6)).astype(bf16)
    h = nn(c, up) + bup
    t = jnp.tanh(h * (K0 + (K0 * K1) * h * h))
    hf = 0.5 + 0.5 * t
    act = (h * hf).astype(bf16)
    dg = (hf + (0.5 * h) * (1.0 - t * t) * (K0 + (3 * K0 * K1) * h * h)).astype(bf16)
    y = (mid + nn(act, down) + row(7)).astype(bf16)
    return y, q, k, v, ctx, lse, mid, act, dg


def plain_bwd(g, x, length, weights, vec, saved):
    mix, out, up, down = weights
    q, k, v, ctx, lse, mid, act, dg = saved
    row = lambda i: vec[i][None]

    def norm_back(dy, src, gain):
        xh, rstd = norm_parts(src)
        e = dy * gain
        d = (e - jnp.mean(e, -1, keepdims=True) - xh * jnp.mean(e * xh, -1, keepdims=True)) * rstd
        return d, jnp.sum(dy * xh, 0), jnp.sum(dy, 0), xh

    def csum(t):
        return jnp.sum(t.astype(f32), 0)

    dh = (nt(g, down) * dg.astype(f32)).astype(bf16)
    d, gain2, shift2, xh2 = norm_back(nt(dh, up), mid, row(5))
    gm = g.astype(f32) + d
    ga = gm.astype(bf16)
    c = (xh2 * row(5) + row(6)).astype(bf16)
    dctx = nt(ga, out).astype(bf16)
    qh, kh, vh, dch = [t.reshape(LEN, D // 64, 64) for t in (q, k, v, dctx)]
    sc = jnp.einsum("qhe,khe->hqk", qh, kh, preferred_element_type=f32)
    pos = jnp.arange(LEN)
    sc = jnp.where(((pos[None, :] <= pos[:, None]) & (pos[None, :] < length[0]))[None], sc, -1e30)
    p = jnp.exp(sc - lse[:, : D // 64].T[:, :, None])
    dp = jnp.einsum("qhe,khe->hqk", dch, vh, preferred_element_type=f32)
    ds = (p * (dp - jnp.sum(p * dp, -1, keepdims=True))).astype(bf16)
    dq = (0.125 * jnp.einsum("hqk,khe->qhe", ds, kh, preferred_element_type=f32)).astype(bf16)
    dk = jnp.einsum("hqk,qhe->khe", ds, qh, preferred_element_type=f32).astype(bf16)
    dv = jnp.einsum("hqk,qhe->khe", p.astype(bf16), dch, preferred_element_type=f32).astype(bf16)
    dm = jnp.concatenate([t.reshape(LEN, D) for t in (dq, dk, dv)], 1)
    xf = x.astype(f32)
    d, gain1, shift1, xh1 = norm_back(nt(dm, mix), xf, row(0))
    a = (xh1 * row(0) + row(1)).astype(bf16)
    rows = [gain1, shift1, csum(dm[:, :D]), csum(dm[:, 2 * D :]), csum(ga), gain2, shift2, csum(g)]
    gv = jnp.concatenate([jnp.stack(rows, 1), csum(dh).reshape(D, FF // D)], 1).reshape(-1)
    return gm + d, (tn(a, dm), tn(ctx, ga), tn(c, dh), tn(act, g), gv)


def plain(lengths, inputs, cotangent, masters, vectors):
    s = lax.axis_index("section")
    length = lax.dynamic_slice_in_dim(lengths, s, 1)
    x0 = lax.dynamic_index_in_dim(inputs, s, 0, keepdims=False)
    cot = lax.dynamic_index_in_dim(cotangent, s, 0, keepdims=False)
    g1 = jnp.where(jnp.arange(LEN, dtype=jnp.int32)[:, None] < length[0], cot, jnp.zeros_like(cot))
    full = [lax.all_gather(m.astype(bf16), "dp", axis=0, tiled=True) for m in masters[:4]]
    full.append(lax.all_gather(vectors[0].astype(bf16), "dp", axis=0, tiled=True))
    full = [jnp.where(s == 0, jnp.stack([w, o]), jnp.stack([o, w])) for w, o in ((w, swap(w)) for w in full)]
    slots = full[4].astype(f32).reshape(2, D, TABLE)
    tables = slots[:, :, :8].transpose(0, 2, 1)
    bups = slots[:, :, 8:].reshape(2, 1, FF)
    weights = [[w[l] for w in full[:4]] for l in range(2)]
    passed, *saved0 = plain_fwd(x0, length, weights[0], tables[0], bups[0])
    final, *saved1 = plain_fwd(passed, length, weights[1], tables[1], bups[1])
    other = swap(jnp.where(s == 0, final, passed))
    acts = jnp.where(s == 0, jnp.stack([passed, other]), jnp.stack([other, final]))
    dx1, grads1 = plain_bwd(g1, passed, length, weights[1], tables[1], saved1)
    dx0, grads0 = plain_bwd(dx1.astype(bf16), x0, length, weights[0], tables[0], saved0)
    other = swap(jnp.where(s == 0, dx1, dx0))
    dxs = jnp.where(s == 0, jnp.stack([dx0, other]), jnp.stack([other, dx1]))
    shards = []
    for a, b in zip(grads0, grads1):
        both = jnp.where(s == 0, a, b) + swap(jnp.where(s == 0, b, a))
        shards.append(lax.psum_scatter(both, "dp", scatter_dimension=0, tiled=True))
    shards[4] = shards[4][None]
    total = jnp.full((8, 128), lax.psum(sum(jnp.sum(g * g) for g in shards), ("section", "dp")))
    return acts, dxs, shards, total


def on_device(inputs, cotangent, lengths, mix, out, up, down, vectors, *moments):
    s = lax.axis_index("section")
    n_dp = lax.axis_size("dp")
    custom = n_dp == ZS * YS * XS
    masters = [m[0] for m in (mix, out, up, down)] + [vectors]
    firsts = [m[0] for m in moments[:4]] + [moments[4]]
    seconds = [m[0] for m in moments[5:9]] + [moments[9]]
    part = vectors.shape[1]
    if custom:
        got = front(lengths, inputs, masters[:4], vectors.reshape(48, TABLE))
        weights, tables, (acts, passed), saved = got[1:NC], got[NC : NC + 2], got[NC + 2 : NC + 4], (got[NC + 4 : NC + 12], got[NC + 12 :])
        dxs, *shards, total = back(lengths, inputs, cotangent, passed, weights, tables, saved)
        shards[4] = shards[4].reshape(1, part)
    else:
        acts, dxs, shards, total = plain(lengths, inputs, cotangent, masters, vectors)
    results = adam(total, shards, masters, firsts, seconds, [acts, dxs])
    results = [r if i >= 12 else r[None] for i, r in enumerate(results[:15])] + list(results[15:])
    return (results[15], results[16], jnp.sqrt(total[0, 0])) + tuple(results[:15])


def solution(mesh):
    rows = P("dp", None, None)
    mats = (P("section", "dp", None),) * 4
    vec = (P("section", "dp"),)
    acts = P("section", "dp", None, None)
    return jax.shard_map(
        on_device,
        mesh=mesh,
        in_specs=(rows, rows, P("dp")) + (mats + vec) * 3,
        out_specs=(acts, acts, P()) + (P("section", "dp", None),) * 12 + vec * 3,
        check_vma=False,
    )
```

```python
import jax, jax.numpy as jnp
from jax import lax
from jax.experimental import pallas as pl
from jax.experimental.pallas import tpu as pltpu
from jax.sharding import PartitionSpec as P
D=768; FF=3072; LEN=1024; RB=256; NB=LEN//RB; FB=768
f32=jnp.float32; bf16=jnp.bfloat16
NT=(((1,),(1,)),((),())); TN=(((0,),(0,)),((),()))
def nn(a,b): return jnp.dot(a,b,preferred_element_type=f32)
def nt(a,b): return lax.dot_general(a,b,NT,preferred_element_type=f32)
def tn(a,b): return lax.dot_general(a,b,TN,preferred_element_type=f32)
K0=0.7978845608028654; K1=0.044715
def rows_of(i): return pl.ds(pl.multiple_of(i*RB,RB),RB)
def norm_parts(v):
    cen=v-jnp.mean(v,-1,keepdims=True)
    rstd=lax.rsqrt(jnp.mean(cen*cen,-1,keepdims=True)+1e-5)
    return cen*rstd, rstd
VM = pl.BlockSpec(memory_space=pltpu.VMEM)
SM = pl.BlockSpec(memory_space=pltpu.SMEM)
AN = pl.BlockSpec(memory_space=pl.ANY)
MESH = pl.DeviceIdType.MESH
MIB = 2**20
STEP = 10
TABLE = 8 + FF // D


def S(shape, dtype):
    return jax.ShapeDtypeStruct(shape, dtype)


def vm_like(items):
    return [pltpu.VMEM(i.shape, i.dtype) for i in items]


def flat(ref, z=None):
    w = ref[...] if z is None else ref[z]
    return w.reshape(-1, w.shape[-1])


def cols(ref, lo, n, l=None):
    w = ref[:, :, :, :, lo : lo + n] if l is None else ref[l, :, :, :, :, lo : lo + n]
    return w.reshape(-1, n)


ZS, YS, XS = 4, 2, 2


def place():
    s = lax.axis_index("section")
    d = lax.axis_index("dp")
    return s, d // (YS * XS), (d // XS) % YS, d % XS


def at_chip(s, z, y, x):
    return (s, z * (YS * XS) + y * XS + x)


def partners(s, z, y, x):
    others = [at_chip(1 - s, z, y, x), at_chip(s, z, y, 1 - x), at_chip(s, z, 1 - y, x)]
    return others + [at_chip(s, (z + r) % ZS, y, x) for r in range(1, ZS)]


def far_plane(s, z, y, x):
    return [at_chip(s, z, 1 - y, 1 - x)] + [at_chip(1 - s, z, yy, xx) for yy, xx in ((y, 1 - x), (1 - y, x), (1 - y, 1 - x))]


def greet(devices):
    barrier = pltpu.get_barrier_semaphore()
    for dev in devices:
        pl.semaphore_signal(barrier, inc=1, device_id=dev, device_id_type=MESH)
    pl.semaphore_wait(barrier, len(devices))


CHUNKS = ("vec", "wq", "wk", "wv", "wo", "u0", "u1", "dA", "dB")
NC = len(CHUNKS)
VL = 384


def mask_table(j):
    row = lax.broadcasted_iota(jnp.int32, (48, VL), 0)
    lane = lax.broadcasted_iota(jnp.int32, (48, VL), 1)
    one = [lane == 48 * (j % 8) + row] + [lane == 192 * (j % 2) + 4 * row + t for t in range(4)]
    return [m.astype(f32).astype(bf16) for m in one]


def front(lengths, inputs, masters, vec48):
    chunk = [(16, VL)] + [(48, D)] * 4 + [(48, FF // 2)] * 2 + [(192, 512), (192, 256)]
    saved = [S((LEN, D), bf16)] * 4 + [S((LEN, 128), f32), S((LEN, D), f32), S((LEN, FF), bf16), S((LEN, FF), bf16)]
    half = ZS // 2

    def kern(len_ref, x_h, mix, out, up, down, v48, *refs):
        full, refs = (None,) + refs[: NC - 1], refs[NC - 1 :]
        tabs, refs = refs[:2], refs[2:]
        (acto, pas), keep, refs = refs[:2], (refs[2:10], refs[10:18]), refs[18:]
        wv, refs = refs[:NC], refs[NC:]
        x0, y0, ab, q, k, v, ctx, lse, mid, act, dg, bup, send, recv, lsem, ksem, asem, arecv = refs
        s, z, y, x = place()
        length = len_ref[s]
        near = partners(s, z, y, x)
        sib, px, py, pz = near[0], near[1], near[2], near[3:]
        x_in = pltpu.make_async_copy(x_h.at[s], x0, lsem.at[0])
        x_in.start()
        greet(near)
        lo, hi = slice(0, half), slice(half, ZS)

        def copy(a, slot, idx, dev):
            dst = wv[a].at[idx]
            return pltpu.make_async_remote_copy(
                src_ref=dst, dst_ref=dst, send_sem=send.at[a, slot],
                recv_sem=recv.at[a, slot], device_id=dev, device_id_type=MESH)

        def prepare(a):
            own = wv[a].at[s, z, y, x]
            if a == 0:
                maps = mask_table((z * YS + y) * XS + x)
                vb = v48[...].astype(bf16)
                ups = sum(tn(vb, maps[1 + t])[8 + t : 9 + t] for t in range(4))
                own[...] = jnp.concatenate([tn(vb, maps[0])[0:8], jnp.broadcast_to(ups, (8, VL))], 0).astype(bf16)
            elif a < 4:
                own[...] = mix[:, (a - 1) * D : a * D].astype(bf16)
            elif a == 4:
                own[...] = out[...].astype(bf16)
            elif a < 7:
                own[...] = up[:, (a - 5) * (FF // 2) : (a - 4) * (FF // 2)].astype(bf16)
            else:
                own[...] = (down[:, 0:512] if a == 7 else down[:, 512:D]).astype(bf16)

        def first(a):
            for r in range(1, ZS):
                copy(a, r - 1, (s, z, y, x), pz[r - 1]).start()

        second_out = [(3, (s, lo, y, x), px), (4, (s, hi, y, x), py)]
        second_in = [(3, (s, lo, y, 1 - x), px), (4, (s, hi, 1 - y, x), py)]
        third_out = [(5, (s, lo, y), py), (6, (s, hi, slice(None), x), px)]
        third_in = [(5, (s, lo, 1 - y), py), (6, (s, hi, slice(None), 1 - x), px)]

        def waves(l):
            return [
                [(7, (l, slice(None), y, x), sib)],
                [(8, (l, lo, y, 1 - x), sib), (9, (l, hi, 1 - y, x), sib)],
                [(10, (l, lo, 1 - y), sib), (11, (l, hi, slice(None), 1 - x), sib)],
            ]

        def second(a):
            for r in range(1, ZS):
                copy(a, r - 1, (s, (z - r) % ZS, y, x), pz[r - 1]).wait_recv()
            for c in second_out + waves(s)[0]:
                copy(a, *c).start()

        def third(a):
            for c in second_in:
                copy(a, *c).wait_recv()
            for c in third_out + waves(s)[1]:
                copy(a, *c).start()

        def last(a):
            for c in third_in:
                copy(a, *c).wait_recv()
            for c in waves(s)[2]:
                copy(a, *c).start()

        seen = set()

        def event(l, *what):
            todo = [w for w in what if (l, w) not in seen and w[1] < NC]
            seen.update((l, w) for w in todo)
            if todo:
                @pl.when(s == l)
                def _():
                    for stage, a in todo:
                        stage(a)

        def group(l, a):
            event(l, (third, a), (second, a + 2))

        def store_w(l, a):
            return pltpu.make_async_copy(wv[a].at[l], full[a].at[l], lsem.at[a])

        def complete(l, a):
            event(l, (last, a))

            @pl.when(s != l)
            def _():
                for wave in waves(l):
                    for c in wave:
                        copy(a, *c).wait_recv()
            if a:
                if l:
                    store_w(0, a).wait()
                store_w(l, a).start()

        def store(l, i):
            if i == 0:
                return pltpu.make_async_copy(y0, pas, ksem.at[0])
            return pltpu.make_async_copy((q, k, v, ctx, lse, mid, act)[i - 1], keep[l][i - 1], ksem.at[i])

        def store_dg(l, j):
            return pltpu.make_async_copy(dg.at[j % 2], keep[l][7].at[:, j * FB : (j + 1) * FB], ksem.at[8 + j % 2])

        def show(l, local):
            src = (y0, x0)[l]
            if local:
                return pltpu.make_async_copy(src, acto.at[s], asem.at[l])
            return pltpu.make_async_remote_copy(
                src_ref=src, dst_ref=acto.at[s], send_sem=asem.at[l], recv_sem=arecv.at[0], device_id=sib, device_id_type=MESH)

        kb = jnp.where(lax.broadcasted_iota(jnp.int32, (1, LEN), 1) < length, 0.0, -1e30).astype(f32)
        tri = lax.broadcasted_iota(jnp.int32, (RB, RB), 1) <= lax.broadcasted_iota(jnp.int32, (RB, RB), 0)
        lane = lax.broadcasted_iota(jnp.int32, (RB, 128), 1)

        def layer(l, xin, yout):
            vec = tabs[l]

            def settle(i):
                if l:
                    store(0, i).wait()

            complete(l, 0)
            pv = wv[0][l].reshape(16, 16, VL).astype(f32)
            vec[:, 0:VL] = sum(pv[j, 0:8] for j in range(8))
            vec[:, VL:D] = sum(pv[j, 0:8] for j in range(8, 16))
            for m in range(8):
                bup[:, m * VL : (m + 1) * VL] = pv[2 * m, 8:16] + pv[2 * m + 1, 8:16]

            def norm1(i, _):
                r = rows_of(i)
                xh, _r = norm_parts(xin[r, :].astype(f32))
                ab[r, :] = (xh * vec[0:1, :] + vec[1:2, :]).astype(bf16)
                return 0

            lax.fori_loop(0, NB, norm1, 0)

            def project(a, dst, f):
                def step(i, _):
                    r = rows_of(i)
                    dst[r, :] = f(nn(ab[r, :], flat(wv[a], l))).astype(bf16)
                    return 0

                lax.fori_loop(0, NB, step, 0)

            complete(l, 1)
            group(l, 3)
            settle(1)
            project(1, q, lambda t: (t + vec[2:3, :]).astype(bf16).astype(f32) * 0.125)
            store(l, 1).start()
            complete(l, 2)
            group(l, 4)
            settle(2)
            project(2, k, lambda t: t)
            store(l, 2).start()
            complete(l, 3)
            group(l, 5)
            settle(3)
            project(3, v, lambda t: t + vec[3:4, :])
            store(l, 3).start()
            settle(4)
            settle(5)
            lse[...] = jnp.zeros_like(lse)

            def att(p, _):
                @pl.when(p == 1)
                def _():
                    group(l, 6)

                @pl.when(p == 2)
                def _():
                    event(l, (last, 4))

                @pl.when(p == 5)
                def _():
                    group(l, 7)
                    event(l, (last, 5))

                c = pl.ds(pl.multiple_of(p * 128, 128), 128)
                for i in range(NB):
                    top = i * RB
                    r = slice(top, top + RB)
                    qp = q[r, c]
                    outs = []
                    ls = []
                    for h in range(2):
                        qh = jnp.where((lane < 64) == (h == 0), qp, jnp.zeros_like(qp))
                        sd = jnp.where(tri, nt(qh, k[r, c]) + kb[:, top : top + RB], -1e30)
                        m = jnp.max(sd, -1, keepdims=True)
                        if i:
                            sl = nt(qh, k[0:top, c]) + kb[:, 0:top]
                            m = jnp.maximum(m, jnp.max(sl, -1, keepdims=True))
                        ed = jnp.exp(sd - m)
                        tot = jnp.sum(ed, -1, keepdims=True)
                        o = nn(ed.astype(bf16), v[r, c])
                        if i:
                            el = jnp.exp(sl - m)
                            tot = tot + jnp.sum(el, -1, keepdims=True)
                            o = o + nn(el.astype(bf16), v[0:top, c])
                        outs.append(o * (1.0 / tot))
                        ls.append(m + jnp.log(tot))
                    ctx[r, c] = jnp.where(lane < 64, outs[0], outs[1]).astype(bf16)
                    lse[r, :] = jnp.where(lane == 2 * p, ls[0], jnp.where(lane == 2 * p + 1, ls[1], lse[r, :]))
                return 0

            lax.fori_loop(0, D // 128, att, 0)
            store(l, 4).start()
            store(l, 5).start()
            if l == 0:
                event(1, *[(first, a) for a in range(NC)])
            complete(l, 4)
            settle(6)

            def middle(i, _):
                r = rows_of(i)
                md = xin[r, :].astype(f32) + nn(ctx[r, :], flat(wv[4], l)) + vec[4:5, :]
                mid[r, :] = md
                xh, _r = norm_parts(md)
                ab[r, :] = (xh * vec[5:6, :] + vec[6:7, :]).astype(bf16)
                return 0

            lax.fori_loop(0, NB, middle, 0)
            store(l, 6).start()
            settle(7)
            for j in range(FF // FB):
                a = 5 + j // 2
                if j % 2 == 0:
                    complete(l, a)
                if j == 1:
                    group(l, 8)
                if l or j > 1:
                    store_dg(l, j).wait()
                off = (j % 2) * FB
                cc = slice(j * FB, (j + 1) * FB)

                def expand(i, _):
                    r = rows_of(i)
                    h = nn(ab[r, :], cols(wv[a], off, FB, l)) + bup[0:1, cc]
                    h2 = h * h
                    t = jnp.tanh(h * (K0 + (K0 * K1) * h2))
                    hf = 0.5 + 0.5 * t
                    act[r, cc] = (h * hf).astype(bf16)
                    dg[j % 2, r, :] = (hf + (0.5 * h) * (1.0 - t * t) * (K0 + (3 * K0 * K1) * h2)).astype(bf16)
                    return 0

                lax.fori_loop(0, NB, expand, 0)
                store_dg(l, j).start()
            store(l, 7).start()
            if l == 0:
                event(1, (second, 0), (second, 1), (second, 2))
            for a, lo_, hi_ in ((7, 0, 512), (8, 512, D)):
                complete(l, a)
                if l == 0:
                    event(1, *([(third, 0), (third, 1), (second, 3)] if a == 7 else [(third, 2), (second, 4)]))

                def contract(i, _):
                    r = rows_of(i)
                    t = mid[r, lo_:hi_] + nn(act[r, :], flat(wv[a], l)) + vec[7:8, lo_:hi_]
                    yout[r, lo_:hi_] = t.astype(bf16)
                    return 0

                lax.fori_loop(0, NB, contract, 0)
            if l == 0:
                store(l, 0).start()

            @pl.when(s == l)
            def _():
                show(l, True).start()

            @pl.when(s != l)
            def _():
                show(l, False).start()

        for a in range(NC):
            prepare(a)
            event(0, (first, a))
        event(0, (second, 0), (second, 1), (second, 2), (third, 0), (third, 1), (second, 3), (third, 2), (second, 4))
        x_in.wait()
        layer(0, x0, y0)
        layer(1, y0, x0)
        store(0, 0).wait()
        for i in range(1, 8):
            store(1, i).wait()
        for j in range(2):
            store_dg(1, j).wait()
        for a in range(1, NC):
            store_w(1, a).wait()
        for l in range(2):
            @pl.when(s == l)
            def _():
                show(l, True).wait()
                show(l, False).wait_recv()

            @pl.when(s != l)
            def _():
                show(l, False).wait_send()
        for a in range(NC):
            for r in range(1, ZS):
                copy(a, r - 1, (s, z, y, x), pz[r - 1]).wait_send()
            for c in second_out + third_out + sum(waves(s), []):
                copy(a, *c).wait_send()

    outs = [S((2, ZS, YS, XS) + c, bf16) for c in chunk[1:]] + [S((8, D), f32)] * 2 + [S((2, LEN, D), bf16), S((LEN, D), bf16)] + saved * 2
    act_ = [S((LEN, D), bf16)] * 3 + saved[:-1] + [S((2, LEN, FB), bf16), S((8, FF), f32)]
    return pl.pallas_call(
        kern,
        out_shape=outs,
        in_specs=[SM, AN] + [VM] * 5,
        out_specs=[AN] * (NC - 1) + [VM] * 2 + [AN] * 18,
        scratch_shapes=vm_like([S((2, ZS, YS, XS) + c, bf16) for c in chunk] + act_)
        + [pltpu.SemaphoreType.DMA((NC, 12)), pltpu.SemaphoreType.DMA((NC, 12)), pltpu.SemaphoreType.DMA((NC,)), pltpu.SemaphoreType.DMA((10,)), pltpu.SemaphoreType.DMA((2,)), pltpu.SemaphoreType.DMA((1,))],
        compiler_params=pltpu.CompilerParams(collective_id=1, has_side_effects=True, vmem_limit_bytes=64 * MIB - 65536),
        name="front",
    )(lengths, inputs, *masters, vec48)


TILES = (4, 2, 2, 1, 1, 1, 1, 1)
NG = len(TILES)


def back(lengths, inputs, cotangent, passed, weights, tables, saved):
    half = ZS // 2
    HW = D // 2
    blk = [(192, HW), (48, D), (48, D)] + [(48, HW)] * 4 + [(8, HW)]
    typ = [bf16] * 7 + [f32]
    sn = ("q", "k", "v", "ctx", "lse", "mid", "act", "dg")

    def kern(len_ref, tab0, tab1, x_h, cot_h, pas_h, *refs):
        wh, refs = dict(zip(CHUNKS[1:], refs[:8])), refs[8:]
        sh, refs = (dict(zip(sn, refs[:8])), dict(zip(sn, refs[8:16]))), refs[16:]
        dxo, fmix, fout, fup, fdown, fvec, total = refs[:7]
        refs = refs[7:]
        u0, u1, dA, dB, wo, dh, gm, mids, g, ga, dctx, t3, lse, dkT, dvT, lT, gvec, gbup = refs[:18]
        refs = refs[18:]
        own, sibs, a2, b2, a3, b3, r4, fs, fr = [refs[k * NG : (k + 1) * NG] for k in range(9)]
        stD, stU, stV, fo, norms, sq, lsem, dsem, drecv, ssem, srecv, send, recv, fsend, frecv, nsend, nrecv, credit = refs[9 * NG :]
        s, z, y, x = place()
        length = len_ref[s]
        near = partners(s, z, y, x) + far_plane(s, z, y, x)
        sib, px, py, pz = near[0], near[1], near[2], near[3:6]
        plane = near[:3] + near[6:]
        lo, hi = slice(0, half), slice(half, ZS)
        wv = dict(u0=u0, u1=u1, dA=dA, dB=dB, wo=wo)
        names = ("dg", "dA", "dB", "u0", "u1", "wo", "lse", "q", "k", "v", "ctx", "x", "wq", "wk", "wv", "a0", "a1", "a2", "a3", "g")
        slot = {n: k for k, n in enumerate(names)}

        def load(l, n):
            if n in wv:
                a, b = wh[n].at[l], wv[n]
            elif n in ("wq", "wk", "wv"):
                a, b = wh[n].at[l], {"wq": u0.at[:, :, :, :, 0:D], "wk": u0.at[:, :, :, :, D : 2 * D], "wv": u1.at[:, :, :, :, 0:D]}[n]
            elif n == "x":
                a, b = (x_h.at[s], pas_h)[l], ga
            elif n == "g":
                a, b = cot_h.at[s], g
            elif n[0] == "a":
                k = int(n[1])
                a, b = sh[l]["act"].at[:, k * D : (k + 1) * D], t3.at[k % 3]
            else:
                a, b = sh[l][n], dict(dg=dh, lse=lse, q=t3.at[0], k=t3.at[1], v=t3.at[2], ctx=t3.at[1])[n]
            return pltpu.make_async_copy(a, b, lsem.at[slot[n]])

        def start(l, *ns):
            for n in ns:
                load(l, n).start()

        def ready(l, *ns):
            for n in ns:
                load(l, n).wait()

        def mid_load(l, i):
            r = pl.ds(pl.multiple_of(i * RB, RB), RB)
            return pltpu.make_async_copy(sh[l]["mid"].at[r, :], mids.at[lax.rem(i, 2)], lsem.at[len(names) + lax.rem(i, 2)])

        start(1, "g", "dg", "dA", "dB", "u0", "u1", "wo", "lse", "a0", "a1", "a2")
        greet(near)

        def copy(a, k, src, dst, dev):
            return pltpu.make_async_remote_copy(
                src_ref=src, dst_ref=dst, send_sem=send.at[a, k], recv_sem=recv.at[a, k], device_id=dev, device_id_type=MESH)

        def give(a, k, dev):
            pl.semaphore_signal(credit.at[a, k], inc=1, device_id=dev, device_id_type=MESH)

        def take(a, *ks):
            for k in ks:
                pl.semaphore_wait(credit.at[a, k], 1)

        def second(a):
            return [copy(a, 0, own[a].at[lo, 1 - y], a2[a], py), copy(a, 1, own[a].at[hi, :, 1 - x], b2[a], px)]

        def third(a):
            return [copy(a, 2, own[a].at[lo, y, 1 - x], a3[a], px), copy(a, 3, own[a].at[hi, 1 - y, x], b3[a], py)]

        def fourth(a):
            return [copy(a, 3 + r, own[a].at[(z + r) % ZS, y, x], r4[a].at[r - 1], pz[r - 1]) for r in range(1, ZS)]

        first_tile = [sum(TILES[:a]) for a in range(NG)]

        def to_sib(a, t, src=None):
            if a == 0:
                src, dst = stD.at[t % 2] if src is None else src, sibs[0].at[t]
            elif a < 3:
                src, dst = stU.at[t % 2] if src is None else src, sibs[a].at[:, :, :, :, t * HW : (t + 1) * HW]
            elif a < 7:
                src, dst = stU.at[a % 2], sibs[a]
            else:
                src, dst = stV, sibs[a]
            n = first_tile[a] + t
            return pltpu.make_async_remote_copy(
                src_ref=src, dst_ref=dst, send_sem=ssem.at[n], recv_sem=srecv.at[n], device_id=sib, device_id_type=MESH)

        def add(ref, idx, other, oidx):
            ref[idx] = ref[idx] + other[oidx]

        def one(l, a):
            for t in range(TILES[a]):
                to_sib(a, t).wait_recv()

            def step(i, _):
                idx = (i // (YS * XS), (i // XS) % YS, i % XS)
                add(own[a], idx, sibs[a], idx)
                return 0

            lax.fori_loop(0, ZS * YS * XS, step, 0)
            if l:
                give(a, 0, sib)
            else:
                take(a, 1, 2)
            for c in second(a):
                c.start()

        def two(l, a):
            for c in second(a):
                c.wait()

            def step(i, _):
                h, k = i // 2, i % 2
                add(own[a], (h, y, k), a2[a], (h, k))
                add(own[a], (half + h, k, x), b2[a], (h, k))
                return 0

            lax.fori_loop(0, half * 2, step, 0)
            if l:
                give(a, 1, py)
                give(a, 2, px)
            else:
                take(a, 3, 4)
            for c in third(a):
                c.start()

        def three(l, a):
            for c in third(a):
                c.wait()

            def step(h, _):
                add(own[a], (h, y, x), a3[a], (h,))
                add(own[a], (half + h, y, x), b3[a], (h,))
                return 0

            lax.fori_loop(0, half, step, 0)
            if l:
                give(a, 3, px)
                give(a, 4, py)
            else:
                take(a, 5, 6, 7)
            for c in fourth(a):
                c.start()

        def put(a, v, h):
            def at(base, n):
                return pl.ds(pl.multiple_of(base + h * n, n), n)

            if a == 0:
                fdown[:, at(0, HW)] = v
            elif a < 3:
                for t in range(2):
                    fup[:, at(((a - 1) * 2 + t) * D, HW)] = v[:, t * HW : (t + 1) * HW]
            elif a == 3:
                fout[:, at(0, HW)] = v
            elif a < 7:
                for t in range(3):
                    fmix[:, at(t * D + (a - 4) * 256, 128)] = v[:, t * 128 : (t + 1) * 128]

        def finish(a):
            return pltpu.make_async_remote_copy(
                src_ref=fs[a], dst_ref=fr[a], send_sem=fsend.at[a], recv_sem=frecv.at[a], device_id=sib, device_id_type=MESH)

        def four(l, a):
            for c in fourth(a):
                c.wait()
            v = own[a][z, y, x].astype(f32)
            for r in range(ZS - 1):
                v = v + r4[a][r].astype(f32)
            if l:
                for r in range(1, ZS):
                    give(a, 4 + r, at_chip(s, (z - r) % ZS, y, x))
            if a < 7:
                sq[...] = sq[...] + jnp.sum(v * v)
            else:
                j = (z * YS + y) * XS + x
                ln = lax.broadcasted_iota(jnp.int32, (8, HW), 1)
                row = lax.broadcasted_iota(jnp.int32, (8, HW), 0)
                mine = ((s == 0) & (ln // 48 == j % 8)) | ((s == 1) & (row == 0) & (ln // 192 == j % 2))
                sq[...] = sq[...] + jnp.sum(jnp.where(mine, v * v, 0.0))

            @pl.when(s == l)
            def _():
                if a < 7:
                    put(a, v, s)
                else:
                    fo[...] = v

            @pl.when(s != l)
            def _():
                fs[a][...] = v
                finish(a).start()

        def event(*todo):
            for l, stage, a in todo:
                stage(l, a)

        kb = jnp.where(lax.broadcasted_iota(jnp.int32, (1, LEN), 1) < length, 0.0, -1e30).astype(f32)
        tri = lax.broadcasted_iota(jnp.int32, (RB, RB), 1) <= lax.broadcasted_iota(jnp.int32, (RB, RB), 0)
        lane = lax.broadcasted_iota(jnp.int32, (RB, 128), 1)

        def cs(t):
            return jnp.sum(t, 0, keepdims=True)

        def parts(v, cut):
            vb = v.astype(bf16)
            a = jnp.concatenate([vb[:, c : c + w] for c, w in cut[0]], 1) if len(cut[0]) > 1 else vb[:, 0:HW]
            b = jnp.concatenate([vb[:, c : c + w] for c, w in cut[1]], 1) if len(cut[1]) > 1 else vb[:, HW:D]
            return jnp.where(s == 0, a, b), jnp.where(s == 0, b, a)

        straight = ([(0, HW)], [(HW, HW)])
        woven = tuple([(256 * t + 128 * h, 128) for t in range(3)] for h in range(2))

        def dx_copy(l, i, local):
            r = slice(i * RB, (i + 1) * RB)
            if local:
                return pltpu.make_async_copy(gm.at[r, :], dxo.at[s, r, :], dsem.at[i])
            return pltpu.make_async_remote_copy(
                src_ref=gm.at[r, :], dst_ref=dxo.at[s, r, :], send_sem=dsem.at[i], recv_sem=drecv.at[i], device_id=sib, device_id_type=MESH)

        def dx_wait(l, i):
            @pl.when(s == l)
            def _():
                dx_copy(l, i, True).wait()

            @pl.when(s != l)
            def _():
                dx_copy(l, i, False).wait_send()

        def at(l, where):
            if l == 0 and where in rest:
                event(*[(1, st, a) for st, a in rest[where]])
            if where in plan:
                event(*[(l, st, a) for st, a in plan[where]])

        plan = {
            "s0": [(one, 0)], "u1": [(two, 0), (one, 1)], "u3": [(one, 2)], "o": [(one, 3)], "p0": [(three, 0)], "p1": [(two, 1)],
            "p2": [(two, 2), (one, 4)], "p3": [(two, 3), (three, 1), (four, 0)], "p4": [(one, 5), (three, 2)],
            "p5": [(two, 4), (three, 3), (four, 1)], "m": [(one, 6), (four, 2)], "r1": [(two, 5), (three, 4), (four, 3)], "r3": [(two, 6), (three, 5), (four, 4)],
        }
        rest = {
            "d1": [(one, 7)], "d3": [(two, 7), (three, 6)], "s1": [(four, 5), (three, 7)], "s2": [(four, 6)], "s3": [(four, 7)],
        }
        ending = [(one, 7), (three, 6), (four, 5), (two, 7), (three, 7), (four, 6), (four, 7)]

        last_send = {}

        def send_tile(l, a, t, key, write):
            if key in last_send:
                to_sib(*last_send[key]).wait_send()
            write()
            if l == 0 and t == 0:
                take(a, 0)
            to_sib(a, t).start()
            last_send[key] = (a, t)

        def layer(l):
            vec = (tab0, tab1)[l]
            gvec[...] = jnp.zeros_like(gvec)
            gbup[...] = jnp.zeros_like(gbup)
            mid_load(l, 0).start()
            if l:
                ready(l, "g")

                def masked(i, _):
                    r = rows_of(i)
                    pos = i * RB + lax.broadcasted_iota(jnp.int32, (RB, D), 0)
                    g[r, :] = jnp.where(pos < length, g[r, :].astype(f32), 0.0).astype(bf16)
                    return 0

                lax.fori_loop(0, NB, masked, 0)
            for t in range(ZS):
                ready(l, "a%d" % t)

                def write(t=t):
                    for m in range(2):
                        mine, other = parts(tn(t3[t % 3, :, m * HW : (m + 1) * HW], g[...]), straight)
                        own[0][t, m] = mine.reshape(2, 192, HW)
                        stD[t % 2, m] = other.reshape(2, 192, HW)

                send_tile(l, 0, t, ("D", t % 2), write)
                if t == 0:
                    start(l, "a3")
                if t == 1:
                    start(l, "ctx")
                at(l, "d%d" % t)
            ready(l, "dg", "dA", "dB", "wo", "u0", "u1")

            def st1(i, _):
                r = rows_of(i)

                @pl.when(i + 1 < NB)
                def _():
                    mid_load(l, i + 1).start()

                gb = g[r, :]
                gf = gb.astype(f32)
                dc = jnp.zeros((RB, D), f32)
                for j in range(FF // FB):
                    cc = slice(j * FB, (j + 1) * FB)
                    d = ((nt(gb[:, 0:512], flat(dA, j)) + nt(gb[:, 512:], flat(dB, j))) * dh[r, cc].astype(f32)).astype(bf16)
                    dh[r, cc] = d
                    gbup[0:1, cc] += cs(d.astype(f32))
                    dc = dc + nt(d, cols((u0, u1)[j // 2], (j % 2) * FB, FB))
                for k in range(NB):
                    @pl.when(i == k)
                    def _(k=k):
                        at(l, "s%d" % k)
                        if l == 0:
                            dx_wait(1, k)
                mid_load(l, i).wait()
                xh, rstd = norm_parts(mids[lax.rem(i, 2)])
                lT[:, r] = (xh * vec[5:6, :] + vec[6:7, :]).T.astype(bf16)
                e = dc * vec[5:6, :]
                gmv = gf + (e - jnp.mean(e, -1, keepdims=True) - xh * jnp.mean(e * xh, -1, keepdims=True)) * rstd
                gm[r, :] = gmv
                gav = gmv.astype(bf16)
                ga[r, :] = gav
                gvec[4:5, :] += cs(gav.astype(f32))
                gvec[5:6, :] += cs(dc * xh)
                gvec[6:7, :] += cs(dc)
                gvec[7:8, :] += cs(gf)
                dctx[r, :] = nt(gav, flat(wo)).astype(bf16)
                return 0

            lax.fori_loop(0, NB, st1, 0)
            if l:
                start(0, "dA", "dB", "wo")
            start(l, "wq", "wk", "wv")
            start(l, "v")
            for t in range(4):
                a = 1 + t // 2

                def write(t=t, a=a):
                    for m in range(2):
                        v = nn(lT[m * HW : (m + 1) * HW, :], dh[:, t * D : (t + 1) * D])
                        mine, other = parts(v, straight)
                        w = slice((t % 2) * HW, (t % 2 + 1) * HW)
                        own[a][2 * m : 2 * m + 2, :, :, :, w] = mine.reshape(2, 2, 2, 48, HW)
                        stU[t % 2, 2 * m : 2 * m + 2] = other.reshape(2, 2, 2, 48, HW)

                send_tile(l, a, t % 2, ("U", t % 2), write)
                at(l, "u%d" % t)
            start(l, "q")
            if l:
                start(0, "dg")
            ready(l, "ctx")

            def write_out():
                for m in range(2):
                    mine, other = parts(tn(t3[1, :, m * HW : (m + 1) * HW], ga[...]), straight)
                    own[3][2 * m : 2 * m + 2] = mine.reshape(2, 2, 2, 48, HW)
                    stU[1, 2 * m : 2 * m + 2] = other.reshape(2, 2, 2, 48, HW)

            send_tile(l, 3, 0, ("U", 1), write_out)
            start(l, "k", "x")
            at(l, "o")
            ready(l, "x")

            def norm1(i, _):
                r = rows_of(i)
                xh, _r = norm_parts(ga[r, :].astype(f32))
                lT[:, r] = (xh * vec[0:1, :] + vec[1:2, :]).T.astype(bf16)
                return 0

            lax.fori_loop(0, NB, norm1, 0)
            ready(l, "q", "k", "v", "lse")

            def pair(p):
                c = pl.ds(pl.multiple_of(p * 128, 128), 128)
                dkT[...] = jnp.zeros_like(dkT)
                dvT[...] = jnp.zeros_like(dvT)
                for i in range(NB):
                    top = i * RB
                    r = slice(top, top + RB)
                    qp = t3[0, r, c]
                    dcp = dctx[r, c]
                    lr = lse[r, :]
                    qT = qp.astype(f32).T.astype(bf16)
                    dcT = dcp.astype(f32).T.astype(bf16)
                    dq = None
                    for h in range(2):
                        sel = (lane < 64) == (h == 0)
                        qh = jnp.where(sel, qp, jnp.zeros_like(qp))
                        dch = jnp.where(sel, dcp, jnp.zeros_like(dcp))
                        ls = jnp.sum(jnp.where(lane == 2 * p + h, lr, 0.0), -1, keepdims=True)
                        hs = slice(h * 64, h * 64 + 64)
                        pd = jnp.exp(jnp.where(tri, nt(qh, t3[1, r, c]) + kb[:, top : top + RB], -1e30) - ls)
                        dpd = nt(dch, t3[2, r, c])
                        delta = jnp.sum(pd * dpd, -1, keepdims=True)
                        if i:
                            plft = jnp.exp(nt(qh, t3[1, 0:top, c]) + kb[:, 0:top] - ls)
                            dpl = nt(dch, t3[2, 0:top, c])
                            delta = delta + jnp.sum(plft * dpl, -1, keepdims=True)
                        dsd = (pd * (dpd - delta)).astype(bf16)
                        dkT[hs, r] += nn(qT[hs], dsd)
                        dvT[hs, r] += nn(dcT[hs], pd.astype(bf16))
                        t = nn(dsd, t3[1, r, c])
                        if i:
                            dsl = (plft * (dpl - delta)).astype(bf16)
                            dkT[hs, 0:top] += nn(qT[hs], dsl)
                            dvT[hs, 0:top] += nn(dcT[hs], plft.astype(bf16))
                            t = t + nn(dsl, t3[1, 0:top, c])
                        dq = t if h == 0 else jnp.where(lane < 64, dq, t)
                    t3[0, r, c] = (dq * 0.125).astype(bf16)
                t3[1, :, c] = dkT[...].T.astype(bf16)
                t3[2, :, c] = dvT[...].T.astype(bf16)

            def two_pairs(kk, _):
                for b in range(2):
                    for k in range(3):
                        @pl.when(kk == k)
                        def _(k=k):
                            at(l, "p%d" % (2 * k + b))
                    pair(2 * kk + b)
                c2 = pl.ds(pl.multiple_of(kk * 256, 256), 256)
                for k in range(3):
                    @pl.when(kk == k)
                    def _(k=k):
                        def write():
                            for m in range(2):
                                v = jnp.concatenate([nn(lT[m * HW : (m + 1) * HW, :], t3[t, :, k * 256 : (k + 1) * 256]) for t in range(3)], 1)
                                mine, other = parts(v, woven)
                                own[4 + k][2 * m : 2 * m + 2] = mine.reshape(2, 2, 2, 48, HW)
                                stU[k % 2, 2 * m : 2 * m + 2] = other.reshape(2, 2, 2, 48, HW)

                        send_tile(l, 4 + k, 0, ("U", k % 2), write)
                return 0

            lax.fori_loop(0, 3, two_pairs, 0)
            at(l, "m")
            ready(l, "wq", "wk", "wv")

            def st3(i, _):
                r = rows_of(i)
                for k in range(NB):
                    @pl.when(i == k)
                    def _(k=k):
                        at(l, "r%d" % k)
                dq, dk, dv = t3[0, r, :], t3[1, r, :], t3[2, r, :]
                gvec[2:3, :] += cs(dq.astype(f32))
                gvec[3:4, :] += cs(dv.astype(f32))
                da = nt(dq, cols(u0, 0, D)) + nt(dk, cols(u0, D, D)) + nt(dv, cols(u1, 0, D))
                xh, rstd = norm_parts(ga[r, :].astype(f32))
                gvec[0:1, :] += cs(da * xh)
                gvec[1:2, :] += cs(da)
                e = da * vec[0:1, :]
                o = gm[r, :] + (e - jnp.mean(e, -1, keepdims=True) - xh * jnp.mean(e * xh, -1, keepdims=True)) * rstd
                gm[r, :] = o
                g[r, :] = o.astype(bf16)
                for k in range(NB):
                    @pl.when((i == k) & (s == l))
                    def _(k=k):
                        dx_copy(l, k, True).start()

                    @pl.when((i == k) & (s != l))
                    def _(k=k):
                        dx_copy(l, k, False).start()
                return 0

            lax.fori_loop(0, NB, st3, 0)
            if l:
                start(0, "u0", "u1", "lse", "a0", "a1", "a2")

            def write_vec():
                for j in range(ZS * YS * XS):
                    idx = (j // 4, (j // 2) % 2, j % 2)
                    tab = gvec[:, (j // 8) * HW : (j // 8 + 1) * HW]
                    ups = jnp.broadcast_to(gbup[0:1, (j // 2) * HW : (j // 2 + 1) * HW], (8, HW))
                    own[7][idx] = jnp.where(s == 0, tab, ups)
                    stV[idx] = jnp.where(s == 0, ups, tab)

            send_tile(l, 7, 0, "V", write_vec)

        sq[...] = jnp.zeros_like(sq)
        layer(1)
        layer(0)
        event(*[(0, st, a) for st, a in ending])
        norms[0] = sq[...]

        def shared(k, dev, into):
            return pltpu.make_async_remote_copy(
                src_ref=norms.at[k], dst_ref=norms.at[into], send_sem=nsend.at[into], recv_sem=nrecv.at[into], device_id=dev, device_id_type=MESH)

        def gathered(k, devs, into):
            cs_ = [shared(k, dev, into + r) for r, dev in enumerate(devs)]
            for c in cs_:
                c.start()
            for c in cs_:
                c.wait()
            t = norms[k]
            for r in range(len(devs)):
                t = t + norms[into + r]
            return t

        norms[1] = gathered(0, plane, 2)
        total[...] = gathered(1, pz, 2 + len(plane))
        for a in range(NG):
            finish(a).wait()
            if a < 7:
                put(a, fr[a][...], 1 - s)
        tab = jnp.where(s == 0, fo[...], fr[7][...])
        ups = jnp.where(s == 0, fr[7][...], fo[...])
        j = (z * YS + y) * XS + x
        row = lax.broadcasted_iota(jnp.int32, (48, HW), 0)
        ln = lax.broadcasted_iota(jnp.int32, (48, HW), 1)
        col = lax.broadcasted_iota(jnp.int32, (48, TABLE), 1)
        vals = jnp.zeros((48, TABLE), f32)
        for k in range(TABLE):
            if k < 8:
                got = jnp.sum(jnp.where(ln == 48 * (j % 8) + row, tab[k : k + 1], 0.0), -1, keepdims=True)
            else:
                got = jnp.sum(jnp.where(ln == 192 * (j % 2) + 4 * row + (k - 8), ups[0:1], 0.0), -1, keepdims=True)
            vals = jnp.where(col == k, got, vals)
        fvec[...] = vals
        for i in range(NB):
            dx_wait(0, i)
            dx_copy(0, i, False).wait_recv()
        for key, (a, t) in last_send.items():
            to_sib(a, t).wait_send()

    def bufs(lead):
        return [S(lead + blk[a], typ[a]) for a in range(NG)]

    w5 = [S(w.shape[1:], bf16) for w in weights]
    work = [w5[4], w5[5], w5[6], w5[7], w5[3], S((LEN, FF), bf16), S((LEN, D), f32), S((2, RB, D), f32)] + [S((LEN, D), bf16)] * 3
    work += [S((3, LEN, D), bf16), S((LEN, 128), f32), S((128, LEN), f32), S((128, LEN), f32), S((D, LEN), bf16), S((8, D), f32), S((8, FF), f32)]
    for lead in ((ZS, YS, XS), (ZS, YS, XS), (half, XS), (half, YS), (half,), (half,), (ZS - 1,)):
        work += bufs(lead)
    work += [S(b, f32) for b in blk] * 2
    work += [S((2, 2, 2, 192, HW), bf16), S((2, ZS, YS, XS, 48, HW), bf16), S((ZS, YS, XS, 8, HW), f32), S((8, HW), f32), S((16, 8, 128), f32), S((8, 128), f32)]
    dma = pltpu.SemaphoreType.DMA
    nt_ = sum(TILES)
    sems = [dma((22,)), dma((NB,)), dma((NB,)), dma((nt_,)), dma((nt_,)), dma((NG, 7)), dma((NG, 7)), dma((NG,)), dma((NG,)), dma((16,)), dma((16,)), pltpu.SemaphoreType.REGULAR((NG, 8))]
    outs = [S((2, LEN, D), f32), S((48, 3 * D), f32), S((48, D), f32), S((48, FF), f32), S((192, D), f32), S((48, TABLE), f32), S((8, 128), f32)]
    return pl.pallas_call(
        kern,
        out_shape=outs,
        in_specs=[SM, VM, VM] + [AN] * 27,
        out_specs=[AN] + [VM] * 6,
        scratch_shapes=vm_like(work) + sems,
        compiler_params=pltpu.CompilerParams(collective_id=2, has_side_effects=True, vmem_limit_bytes=64 * MIB - 65536),
        name="back",
    )(lengths, *tables, inputs, cotangent, passed, *weights, *saved[0], *saved[1])


RATES = (0.05, 0.25, 0.05, 0.05, 0.5)
DECAYS = (0.1, 0.1, 0.1, 0.1, 0.0)


def adam(total, grads, masters, firsts, seconds, whole):
    n = len(grads)
    flat_ = [a for four in zip(grads, masters, firsts, seconds) for a in four]
    steps = 6
    nw = len(whole)

    def spec(a):
        if a.shape[0] % (8 * steps):
            return pl.BlockSpec(a.shape, lambda i: (0, 0))
        return pl.BlockSpec((a.shape[0] // steps, a.shape[1]), lambda i: (i, 0))

    def kern(t, *refs):
        src, refs = refs[:nw], refs[nw:]
        ins, refs = refs[: 4 * n], refs[4 * n :]
        outs, dst, refs = refs[: 3 * n], refs[3 * n : 3 * n + nw], refs[3 * n + nw :]
        hold, sem = refs[:nw], refs[nw]
        into = [pltpu.make_async_copy(src[i], hold[i], sem.at[i]) for i in range(nw)]
        cps = [pltpu.make_async_copy(hold[i], dst[i].at[0], sem.at[i]) for i in range(nw)]

        @pl.when(pl.program_id(0) == 0)
        def _():
            for c in into:
                c.start()

        @pl.when(pl.program_id(0) == 2)
        def _():
            for i in range(nw):
                into[i].wait()
                cps[i].start()

        norm = jnp.sqrt(t[0:1, 0:1])
        factor = jnp.minimum(1.0, 1.0 / (norm + 1e-06))
        for i in range(n):
            gr, w, m, u = (r[...] for r in ins[4 * i : 4 * i + 4])
            mo, uo, wo = outs[3 * i : 3 * i + 3]
            gr = gr * factor
            m1 = 0.9 * m + (1.0 - 0.9) * gr
            u1 = 0.999 * u + (1.0 - 0.999) * gr * gr
            mh = m1 / (1.0 - 0.9**STEP)
            uh = u1 / (1.0 - 0.999**STEP)
            mo[...] = m1
            uo[...] = u1
            wo[...] = w - RATES[i] * (mh / (jnp.sqrt(uh) + 1e-08) + DECAYS[i] * w)

        @pl.when(pl.program_id(0) == steps - 1)
        def _():
            for c in cps:
                c.wait()

    outs = [S(a.shape, f32) for a in masters for _ in range(3)]
    return pl.pallas_call(
        kern,
        grid=(steps,),
        out_shape=outs + [S((1,) + w.shape, w.dtype) for w in whole],
        in_specs=[pl.BlockSpec((8, 128), lambda i: (0, 0))] + [AN] * nw + [spec(a) for a in flat_],
        out_specs=[spec(a) for a in outs] + [AN] * nw,
        scratch_shapes=vm_like(whole) + [pltpu.SemaphoreType.DMA((nw,))],
        compiler_params=pltpu.CompilerParams(vmem_limit_bytes=62 * MIB),
        name="adam",
    )(total, *whole, *flat_)


def swap(v):
    return lax.ppermute(v, "section", [(0, 1), (1, 0)])


def plain_fwd(x, length, weights, vec, bup):
    mix, out, up, down = weights
    row = lambda i: vec[i][None]
    xf = x.astype(f32)
    a = (norm_parts(xf)[0] * row(0) + row(1)).astype(bf16)
    m = nn(a, mix)
    q = ((m[:, :D] + row(2)).astype(bf16).astype(f32) * 0.125).astype(bf16)
    k = m[:, D : 2 * D].astype(bf16)
    v = (m[:, 2 * D :] + row(3)).astype(bf16)
    heads = [t.reshape(LEN, D // 64, 64) for t in (q, k, v)]
    sc = jnp.einsum("qhe,khe->hqk", heads[0], heads[1], preferred_element_type=f32)
    pos = jnp.arange(LEN)
    sc = jnp.where(((pos[None, :] <= pos[:, None]) & (pos[None, :] < length[0]))[None], sc, -1e30)
    top = jnp.max(sc, -1, keepdims=True)
    e = jnp.exp(sc - top)
    tot = jnp.sum(e, -1, keepdims=True)
    ctx = jnp.einsum("hqk,khe->qhe", (e / tot).astype(bf16), heads[2], preferred_element_type=f32).reshape(LEN, D).astype(bf16)
    lse = jnp.pad((top + jnp.log(tot))[:, :, 0].T, ((0, 0), (0, 128 - D // 64)))
    mid = xf + nn(ctx, out) + row(4)
    c = (norm_parts(mid)[0] * row(5) + row(6)).astype(bf16)
    h = nn(c, up) + bup
    t = jnp.tanh(h * (K0 + (K0 * K1) * h * h))
    hf = 0.5 + 0.5 * t
    act = (h * hf).astype(bf16)
    dg = (hf + (0.5 * h) * (1.0 - t * t) * (K0 + (3 * K0 * K1) * h * h)).astype(bf16)
    y = (mid + nn(act, down) + row(7)).astype(bf16)
    return y, q, k, v, ctx, lse, mid, act, dg


def plain_bwd(g, x, length, weights, vec, saved):
    mix, out, up, down = weights
    q, k, v, ctx, lse, mid, act, dg = saved
    row = lambda i: vec[i][None]

    def norm_back(dy, src, gain):
        xh, rstd = norm_parts(src)
        e = dy * gain
        d = (e - jnp.mean(e, -1, keepdims=True) - xh * jnp.mean(e * xh, -1, keepdims=True)) * rstd
        return d, jnp.sum(dy * xh, 0), jnp.sum(dy, 0), xh

    def csum(t):
        return jnp.sum(t.astype(f32), 0)

    dh = (nt(g, down) * dg.astype(f32)).astype(bf16)
    d, gain2, shift2, xh2 = norm_back(nt(dh, up), mid, row(5))
    gm = g.astype(f32) + d
    ga = gm.astype(bf16)
    c = (xh2 * row(5) + row(6)).astype(bf16)
    dctx = nt(ga, out).astype(bf16)
    qh, kh, vh, dch = [t.reshape(LEN, D // 64, 64) for t in (q, k, v, dctx)]
    sc = jnp.einsum("qhe,khe->hqk", qh, kh, preferred_element_type=f32)
    pos = jnp.arange(LEN)
    sc = jnp.where(((pos[None, :] <= pos[:, None]) & (pos[None, :] < length[0]))[None], sc, -1e30)
    p = jnp.exp(sc - lse[:, : D // 64].T[:, :, None])
    dp = jnp.einsum("qhe,khe->hqk", dch, vh, preferred_element_type=f32)
    ds = (p * (dp - jnp.sum(p * dp, -1, keepdims=True))).astype(bf16)
    dq = (0.125 * jnp.einsum("hqk,khe->qhe", ds, kh, preferred_element_type=f32)).astype(bf16)
    dk = jnp.einsum("hqk,qhe->khe", ds, qh, preferred_element_type=f32).astype(bf16)
    dv = jnp.einsum("hqk,qhe->khe", p.astype(bf16), dch, preferred_element_type=f32).astype(bf16)
    dm = jnp.concatenate([t.reshape(LEN, D) for t in (dq, dk, dv)], 1)
    xf = x.astype(f32)
    d, gain1, shift1, xh1 = norm_back(nt(dm, mix), xf, row(0))
    a = (xh1 * row(0) + row(1)).astype(bf16)
    rows = [gain1, shift1, csum(dm[:, :D]), csum(dm[:, 2 * D :]), csum(ga), gain2, shift2, csum(g)]
    gv = jnp.concatenate([jnp.stack(rows, 1), csum(dh).reshape(D, FF // D)], 1).reshape(-1)
    return gm + d, (tn(a, dm), tn(ctx, ga), tn(c, dh), tn(act, g), gv)


def plain(lengths, inputs, cotangent, masters, vectors):
    s = lax.axis_index("section")
    length = lax.dynamic_slice_in_dim(lengths, s, 1)
    x0 = lax.dynamic_index_in_dim(inputs, s, 0, keepdims=False)
    cot = lax.dynamic_index_in_dim(cotangent, s, 0, keepdims=False)
    g1 = jnp.where(jnp.arange(LEN, dtype=jnp.int32)[:, None] < length[0], cot, jnp.zeros_like(cot))
    full = [lax.all_gather(m.astype(bf16), "dp", axis=0, tiled=True) for m in masters[:4]]
    full.append(lax.all_gather(vectors[0].astype(bf16), "dp", axis=0, tiled=True))
    full = [jnp.where(s == 0, jnp.stack([w, o]), jnp.stack([o, w])) for w, o in ((w, swap(w)) for w in full)]
    slots = full[4].astype(f32).reshape(2, D, TABLE)
    tables = slots[:, :, :8].transpose(0, 2, 1)
    bups = slots[:, :, 8:].reshape(2, 1, FF)
    weights = [[w[l] for w in full[:4]] for l in range(2)]
    passed, *saved0 = plain_fwd(x0, length, weights[0], tables[0], bups[0])
    final, *saved1 = plain_fwd(passed, length, weights[1], tables[1], bups[1])
    other = swap(jnp.where(s == 0, final, passed))
    acts = jnp.where(s == 0, jnp.stack([passed, other]), jnp.stack([other, final]))
    dx1, grads1 = plain_bwd(g1, passed, length, weights[1], tables[1], saved1)
    dx0, grads0 = plain_bwd(dx1.astype(bf16), x0, length, weights[0], tables[0], saved0)
    other = swap(jnp.where(s == 0, dx1, dx0))
    dxs = jnp.where(s == 0, jnp.stack([dx0, other]), jnp.stack([other, dx1]))
    shards = []
    for a, b in zip(grads0, grads1):
        both = jnp.where(s == 0, a, b) + swap(jnp.where(s == 0, b, a))
        shards.append(lax.psum_scatter(both, "dp", scatter_dimension=0, tiled=True))
    shards[4] = shards[4][None]
    total = jnp.full((8, 128), lax.psum(sum(jnp.sum(g * g) for g in shards), ("section", "dp")))
    return acts, dxs, shards, total


def on_device(inputs, cotangent, lengths, mix, out, up, down, vectors, *moments):
    s = lax.axis_index("section")
    n_dp = lax.axis_size("dp")
    custom = n_dp == ZS * YS * XS
    masters = [m[0] for m in (mix, out, up, down)] + [vectors]
    firsts = [m[0] for m in moments[:4]] + [moments[4]]
    seconds = [m[0] for m in moments[5:9]] + [moments[9]]
    part = vectors.shape[1]
    if custom:
        got = front(lengths, inputs, masters[:4], vectors.reshape(48, TABLE))
        weights, got = got[: NC - 1], got[NC - 1 :]
        tables, (acts, passed), saved = got[:2], got[2:4], (got[4:12], got[12:])
        dxs, *shards, total = back(lengths, inputs, cotangent, passed, weights, tables, saved)
        shards[4] = shards[4].reshape(1, part)
    else:
        acts, dxs, shards, total = plain(lengths, inputs, cotangent, masters, vectors)
    results = adam(total, shards, masters, firsts, seconds, [acts, dxs])
    results = [r if i >= 12 else r[None] for i, r in enumerate(results[:15])] + list(results[15:])
    return (results[15], results[16], jnp.sqrt(total[0, 0])) + tuple(results[:15])


def solution(mesh):
    rows = P("dp", None, None)
    mats = (P("section", "dp", None),) * 4
    vec = (P("section", "dp"),)
    acts = P("section", "dp", None, None)
    return jax.shard_map(
        on_device,
        mesh=mesh,
        in_specs=(rows, rows, P("dp")) + (mats + vec) * 3,
        out_specs=(acts, acts, P()) + (P("section", "dp", None),) * 12 + vec * 3,
        check_vma=False,
    )
```
